32 devices in a mesh: gx: 8 (over z, x), gy: 4 (over y, core).
Axes of the slice: x: 2, y: 2, z: 4, core: 2. Of those that a mesh axis runs over, the one named last changes fastest.
Arguments:
- disp: float32 [2, 64, 4096], P(None, 'gx', 'gy'), may hold values from -0.2 to 0.2
- vel: float32 [2, 64, 4096], P(None, 'gx', 'gy'), may hold values from -1 to 1
- bonds: int32 [4, 64, 4096], P(None, 'gx', 'gy'), may hold values from 0 to 127, as said below
Outputs:
- new_disp: float32 [2, 64, 4096], P(None, 'gx', 'gy')
- new_vel: float32 [2, 64, 4096], P(None, 'gx', 'gy')
The draws below stay inside these ranges and needn't reach their ends.
Inputs may be any that keep to these rules, and one draw needn't show every extreme that they name: `bonds`: bit j of word 0 is bit j of the table's word 0 (j < 3), bits 0 to 6 of words 1 to 3 likewise; word 0 is below 8 and no higher bits are set.
All inputs are finite; a program needn't handle non-finite values.
Results may differ from the reference program's by a relative error of at most 0.00002.
Values sent between devices are 32-bit elements; how exact they have to be, the bound alone decides.
A program may use at most 64 MiB of HBM per device.

```python
import math
import jax
import jax.numpy as jnp

STEPS = 2
NX = 64
NY = 4096


def draw_bonds(key, part):
    subkeys = jax.random.split(key, 3)
    grid_shape = (4, NX, NY)
    draw_one = jax.random.randint(subkeys[0], grid_shape, 0, 128)
    draw_two = jax.random.randint(subkeys[1], grid_shape, 0, 128)
    draw_three = jax.random.randint(subkeys[2], grid_shape, 0, 128)
    packed = jnp.bitwise_or(jnp.bitwise_or(draw_one, draw_two), draw_three)
    ceiling = jnp.where(jnp.arange(4)[:, None, None] == 0, 7, 127).astype(jnp.int32)
    return jnp.bitwise_and(packed, ceiling).astype(jnp.int32)


def level_of(rng, dims, cuts, least, high):
    factor_of = 1.0
    for dim, blocks in cuts:
        steps = jax.random.uniform(jax.random.fold_in(jax.random.fold_in(rng, 6), dim), (blocks,), jnp.float32, least / len(cuts), high / len(cuts))
        factor_of = factor_of * jnp.repeat(jnp.exp(steps), dims[dim] // blocks).reshape((-1,) + (1,) * (len(dims) - 1 - dim))
    return factor_of


def setup_inputs(seed: int = 0) -> dict:
    key_of = jax.random.split(jax.random.key(seed), 4)
    return {
        "disp": jnp.clip(jax.random.uniform(key_of[0], (2, NX, NY), jnp.float32, -0.2, 0.2) * level_of(key_of[0], (2, NX, NY), ((1, 8), (2, 4)), -0.4, 0.0), -0.2, 0.2),
        "vel": jnp.clip(jax.random.uniform(key_of[1], (2, NX, NY), jnp.float32, -1.0, 1.0) * level_of(key_of[1], (2, NX, NY), ((1, 8), (2, 4)), -0.4, 0.0), -1.0, 1.0),
        "bonds": draw_bonds(jax.random.fold_in(key_of[3], 71), 0),
    }


STIFFNESS = 40.0
DAMPING = 1.0
TIME_STEP = 0.05
SOFTENING = 0.0625
BOND_TABLE = [(0, c, 0, c - 1) for c in (1, 2, 3)] + [(r, c, r, c + 3) for r in (1, 2, 3) for c in (-3, -2, -1, 0, 1, 2, 3)]

def bond_force(near_state, far_state, row_off, col_off, intact):
    length = math.sqrt(row_off * row_off + col_off * col_off)
    rest = math.sqrt(length * length + SOFTENING)
    along_x = row_off + far_state[0] - near_state[0]
    along_y = col_off + far_state[1] - near_state[1]
    stretched = jnp.sqrt(along_x * along_x + along_y * along_y + SOFTENING)
    strain = (stretched - rest) / length
    closing = (along_x * (far_state[2] - near_state[2]) + along_y * (far_state[3] - near_state[3])) / (stretched * length)
    tension = intact * (STIFFNESS * strain + DAMPING * closing) / length
    return (tension * along_x / stretched, tension * along_y / stretched)

def intact_bits(word_array, bit):
    return jnp.bitwise_and(jnp.right_shift(word_array, bit), 1).astype(jnp.float32)

def total_force(state, bonds):
    force_x = jnp.zeros(state.shape[1:], jnp.float32)
    force_y = jnp.zeros(state.shape[1:], jnp.float32)
    for row_off, col_off, word, bit in BOND_TABLE:
        far_state = jnp.roll(state, (-row_off, -col_off), axis=(1, 2))
        pull_x, pull_y = bond_force(state, far_state, row_off, col_off, intact_bits(bonds[word], bit))
        force_x = force_x + pull_x - jnp.roll(pull_x, (row_off, col_off), axis=(0, 1))
        force_y = force_y + pull_y - jnp.roll(pull_y, (row_off, col_off), axis=(0, 1))
    return jnp.stack([force_x, force_y])

def reference(disp, vel, bonds):
    acceleration = total_force(jnp.concatenate([disp, vel], 0), bonds)
    for step in range(STEPS):
        half_vel = vel + 0.5 * TIME_STEP * acceleration
        disp = disp + TIME_STEP * half_vel
        acceleration = total_force(jnp.concatenate([disp, half_vel], 0), bonds)
        vel = half_vel + 0.5 * TIME_STEP * acceleration
    return (disp, vel)
```

```python
import functools
import math

import jax
import jax.numpy as jnp
from jax import lax
from jax.experimental import pallas as pl
from jax.experimental.pallas import tpu as pltpu
from jax.sharding import PartitionSpec as P

STEPS = 2
STIFFNESS = 40.0
DAMPING = 1.0
TIME_STEP = 0.05
SOFTENING = 0.0625
REACH = 3
LANES = 128
GROUP = 2
PACK = (1, 8, 1024, 131072)
PACK_SHIFT = (0, 3, 10, 17)
MESH = pl.DeviceIdType.MESH
SHIFTS = tuple(range(-REACH, REACH + 1))


def bond_bit(a, b):
    return b - 1 if a == 0 else PACK_SHIFT[a] + b + REACH


OFFSETS = [(a, b) for a in SHIFTS for b in SHIFTS if (a, b) != (0, 0)]


def in_table(a, b):
    return a > 0 or (a == 0 and b > 0)


def shifted(x, low, high, b, segment, lane):
    segments = x.shape[0]
    if b > 0:
        after = jnp.where(segment == segments - 1, high, pltpu.roll(x, segments - 1, 0))
        return pltpu.roll(jnp.where(lane < b, after, x), LANES - b, 1)
    before = jnp.where(segment == 0, low, pltpu.roll(x, 1, 0))
    return pltpu.roll(jnp.where(lane >= LANES + b, before, x), -b, 1)


def kernel(
    disp_ref, vel_ref, bonds_ref, disp_out, vel_out,
    state, far, half, packed, masks, bond_rows, edge_out, edges_out,
    rows_in, row_bonds_in, edge_in, rows_next, edges_next, send, recv,
):
    rows = disp_ref.shape[1]
    segments = disp_ref.shape[2] // LANES
    gx, gy = lax.axis_index("gx"), lax.axis_index("gy")
    nx, ny = lax.axis_size("gx"), lax.axis_size("gy")
    gx_at = {-1: lax.rem(gx + nx - 1, nx), 0: gx, 1: lax.rem(gx + 1, nx)}
    gy_at = {-1: lax.rem(gy + ny - 1, ny), 0: gy, 1: lax.rem(gy + 1, ny)}
    around = [(x, y) for x in (-1, 0, 1) for y in (-1, 0, 1) if (x, y) != (0, 0)]

    barrier = pltpu.get_barrier_semaphore()
    for x, y in around:
        pl.semaphore_signal(
            barrier, inc=1, device_id=(gx_at[x], gy_at[y]), device_id_type=MESH
        )

    def by_segments(block):
        return block.reshape(rows, segments, LANES)

    last = (segments - 1) * LANES
    for f in range(2):
        for source, plane in ((disp_ref, f), (vel_ref, 2 + f)):
            state[plane] = by_segments(source[f])
            edge_out[0, plane] = source[f, :, 0:LANES]
            edge_out[1, plane] = source[f, :, last : last + LANES]
    words = []
    for w in range(4):
        word = bonds_ref[w].astype(jnp.float32)
        edge_out[0, 4 + w] = word[:, 0:LANES]
        edge_out[1, 4 + w] = word[:, last : last + LANES]
        words.append(by_segments(word))
    slot = 0
    row_bond_slots = {}
    for a in range(1, REACH + 1):
        for r in range(rows - a, rows):
            bond_rows[slot] = words[a][r]
            row_bond_slots[(a, r - rows)] = slot
            slot += 1
    own_packed = words[0] * PACK[0] + words[1] * PACK[1] + words[2] * PACK[2] + words[3] * PACK[3]
    packed[REACH, REACH : REACH + rows] = own_packed.astype(jnp.int32)

    def copy(phase, index, src, dst, x, y):
        return pltpu.make_async_remote_copy(
            src_ref=src, dst_ref=dst, send_sem=send.at[phase, index],
            recv_sem=recv.at[phase, index], device_id=(gx_at[x], gy_at[y]), device_id_type=MESH,
        )

    def copies(phase):
        if phase == 0:
            row_src, row_dst = state, rows_in
        else:
            row_src, row_dst = half.at[phase - 1], rows_next.at[phase - 1]
        out = {
            "down": copy(
                phase, 0, row_src.at[:, rows - REACH : rows], row_dst.at[0], 1, 0
            ),
            "up": copy(phase, 1, row_src.at[:, 0:REACH], row_dst.at[1], -1, 0),
        }
        if phase == 0:
            out["bonds"] = copy(phase, 2, bond_rows, row_bonds_in, 1, 0)
        index = 3
        for side in (0, 1):
            for slot, x in enumerate((1, 0, -1)):
                if phase == 0:
                    planes = 4 if x < 0 else 8
                    src = edge_out.at[side, 0:planes]
                    dst = edge_in.at[1 - side, slot, 0:planes]
                else:
                    src = edges_out.at[phase - 1, side]
                    dst = edges_next.at[phase - 1, 1 - side, slot]
                out[(side, x)] = copy(phase, index, src, dst, x, 2 * side - 1)
                index += 1
        return out

    pl.semaphore_wait(barrier, len(around))
    sent = [copies(0)]
    for c in sent[0].values():
        c.start()

    segment = lax.broadcasted_iota(jnp.int32, (segments, LANES), 0)
    lane = lax.broadcasted_iota(jnp.int32, (segments, LANES), 1)

    def edge_row(r):
        if r < REACH:
            return 0, rows - REACH + r
        if r < REACH + rows:
            return 1, r - REACH
        return 2, r - REACH - rows

    def wait_mid(phase):
        for side in (0, 1):
            sent[phase][(side, 0)].wait_recv()

    def wait_rest(phase):
        for key, c in sent[phase].items():
            if key not in ((0, 0), (1, 0)):
                c.wait_recv()

    def place(plane, r, x, low, high, phase):
        for b in SHIFTS:
            value = x if b == 0 else shifted(x, low, high, b, segment, lane)
            if phase == 0:
                far[plane, b + REACH, r] = value + b if plane == 1 and b else value
            else:
                far[2 + plane, b + REACH, r] = value
                far[plane, b + REACH, r] += TIME_STEP * value

    def place_rows(phase, wanted):
        for r in wanted:
            slot, e = edge_row(r)
            for plane in range(4 if phase == 0 else 2):
                if phase == 0:
                    row_from, edge_from = rows_in, edge_in
                    own = state[plane, r - REACH] if slot == 1 else None
                else:
                    row_from, edge_from = rows_next.at[phase - 1], edges_next.at[phase - 1]
                    own = half[phase - 1, plane, r - REACH] if slot == 1 else None
                if slot == 0:
                    own = row_from[0, plane, r]
                elif slot == 2:
                    own = row_from[1, plane, r - REACH - rows]
                low = edge_from[0, slot, plane, e : e + 1, :]
                high = edge_from[1, slot, plane, e : e + 1, :]
                place(plane, r, own, low, high, phase)

    def place_packed(wanted):
        for r in wanted:
            slot, e = edge_row(r)
            if slot == 0:
                x = jnp.zeros((segments, LANES), jnp.float32)
                for a in range(1, REACH + 1):
                    if (a, r - REACH) in row_bond_slots:
                        x = x + row_bonds_in[row_bond_slots[(a, r - REACH)]] * PACK[a]
                x = x.astype(jnp.int32)
                packed[REACH, r] = x
            else:
                x = packed[REACH, r]
            outer = []
            for side in (0, 1):
                value = edge_in[side, slot, 4, e : e + 1, :]
                for w in range(1, 4):
                    value = value + edge_in[side, slot, 4 + w, e : e + 1, :] * PACK[w]
                outer.append(value.astype(jnp.int32))
            for b in SHIFTS:
                if b:
                    packed[b + REACH, r] = shifted(x, outer[0], outer[1], b, segment, lane)

    def set_masks(index, a, b, first, count):
        scale = 1.0 / (a * a + b * b)
        if in_table(a, b):
            word = packed[REACH, first + REACH : first + REACH + count]
            bit = bond_bit(a, b)
        else:
            word = packed[b + REACH, first + REACH + a : first + REACH + a + count]
            bit = bond_bit(-a, -b)
        masks[index, first : first + count] = jnp.where(
            jnp.bitwise_and(word, 1 << bit) != 0, scale, 0.0
        )

    own_rows = range(REACH, REACH + rows)
    outer_rows = [*range(REACH), *range(REACH + rows, rows + 2 * REACH)]

    for index, (a, b) in enumerate(OFFSETS):
        if in_table(a, b):
            set_masks(index, a, b, 0, rows)
    wait_mid(0)
    place_rows(0, own_rows)
    place_packed(own_rows)
    for index, (a, b) in enumerate(OFFSETS):
        if not in_table(a, b):
            set_masks(index, a, b, -a, rows + a)
    wait_rest(0)
    place_rows(0, outer_rows)
    place_packed(range(REACH))
    for index, (a, b) in enumerate(OFFSETS):
        if a < 0:
            set_masks(index, a, b, 0, -a)

    def forces(phase):
        @pl.loop(0, rows // GROUP)
        def _(group):
            top = group * GROUP
            near = [far[f, REACH, pl.ds(top + REACH, GROUP)] for f in range(4)]
            force_x = jnp.zeros((GROUP, segments, LANES), jnp.float32)
            force_y = jnp.zeros((GROUP, segments, LANES), jnp.float32)
            for index, (a, b) in enumerate(OFFSETS):
                at = pl.ds(top + (REACH + a), GROUP)
                if b == -REACH:
                    near_x = near[0] - float(a)
                rest = STIFFNESS * math.sqrt(a * a + b * b + SOFTENING)
                along_x = far[0, b + REACH, at] - near_x
                along_y = far[1, b + REACH, at] - near[1]
                speed_x = far[2, b + REACH, at] - near[2]
                speed_y = far[3, b + REACH, at] - near[3]
                inverse = lax.rsqrt(along_x * along_x + (along_y * along_y + SOFTENING))
                closing = (along_x * speed_x + along_y * speed_y) * inverse
                if DAMPING != 1.0:
                    closing = closing * DAMPING
                tension = masks[index, pl.ds(top, GROUP)] * (
                    STIFFNESS - inverse * (rest - closing)
                )
                force_x += tension * along_x
                force_y += tension * along_y
            own = pl.ds(top, GROUP)
            for f, force in enumerate((force_x, force_y)):
                kick = (0.5 * TIME_STEP) * force
                value = near[2 + f] + kick
                if 0 < phase < STEPS:
                    value = value + kick
                half[phase, f, own] = value

    for phase in range(STEPS):
        forces(phase)
        for f in range(2):
            for r in range(rows):
                value = half[phase, f, r]
                edges_out[phase, 0, f, r : r + 1, :] = value[0:1]
                edges_out[phase, 1, f, r : r + 1, :] = value[segments - 1 : segments]
        sent.append(copies(phase + 1))
        for c in sent[phase + 1].values():
            c.start()
        wait_mid(phase + 1)
        place_rows(phase + 1, own_rows)
        wait_rest(phase + 1)
        place_rows(phase + 1, outer_rows)
    forces(STEPS)
    for f in range(2):
        disp_out[f] = far[f, REACH, REACH : REACH + rows].reshape(rows, segments * LANES)
        vel_out[f] = half[STEPS, f].reshape(rows, segments * LANES)
    for phase in sent:
        for c in phase.values():
            c.wait_send()


def per_device(disp, vel, bonds):
    rows, columns = disp.shape[1:]
    segments = columns // LANES
    padded = rows + 2 * REACH
    vmem = lambda *shape: pltpu.VMEM(shape, jnp.float32)
    bond_slots = REACH * (REACH + 1) // 2
    spec = pl.BlockSpec(memory_space=pltpu.VMEM)
    return pl.pallas_call(
        kernel,
        out_shape=(jax.ShapeDtypeStruct(disp.shape, disp.dtype),) * 2,
        in_specs=[spec] * 3,
        out_specs=(spec,) * 2,
        scratch_shapes=[
            vmem(4, rows, segments, LANES),
            vmem(4, len(SHIFTS), padded, segments, LANES),
            vmem(STEPS + 1, 2, rows, segments, LANES),
            pltpu.VMEM((len(SHIFTS), REACH + rows, segments, LANES), jnp.int32),
            vmem(len(OFFSETS), rows, segments, LANES),
            vmem(bond_slots, segments, LANES),
            vmem(2, 8, rows, LANES),
            vmem(STEPS, 2, 2, rows, LANES),
            vmem(2, 4, REACH, segments, LANES),
            vmem(bond_slots, segments, LANES),
            vmem(2, 3, 8, rows, LANES),
            vmem(STEPS, 2, 2, REACH, segments, LANES),
            vmem(STEPS, 2, 3, 2, rows, LANES),
            pltpu.SemaphoreType.DMA((STEPS + 1, 9)),
            pltpu.SemaphoreType.DMA((STEPS + 1, 9)),
        ],
        compiler_params=pltpu.CompilerParams(
            collective_id=0, has_side_effects=True, vmem_limit_bytes=32 * 1024 * 1024
        ),
    )(disp, vel, bonds)


def solution(mesh):
    spec = P(None, "gx", "gy")
    return jax.shard_map(
        per_device, mesh=mesh, in_specs=(spec,) * 3, out_specs=(spec,) * 2, check_vma=False
    )
```

```python
import functools
import math

import jax
import jax.numpy as jnp
from jax import lax
from jax.experimental import pallas as pl
from jax.experimental.pallas import tpu as pltpu
from jax.sharding import PartitionSpec as P

STEPS = 2
STIFFNESS = 40.0
DAMPING = 1.0
TIME_STEP = 0.05
SOFTENING = 0.0625
REACH = 3
LANES = 128
GROUP = 2
PACK = (1, 8, 1024, 131072)
PACK_SHIFT = (0, 3, 10, 17)
MESH = pl.DeviceIdType.MESH
SHIFTS = tuple(range(-REACH, REACH + 1))


def bond_bit(a, b):
    return b - 1 if a == 0 else PACK_SHIFT[a] + b + REACH


OFFSETS = [(a, b) for a in SHIFTS for b in SHIFTS if (a, b) != (0, 0)]


def in_table(a, b):
    return a > 0 or (a == 0 and b > 0)


def spread(x, low, high, segment, lane):
    segments = x.shape[0]
    after = jnp.where(segment == segments - 1, high, pltpu.roll(x, segments - 1, 0))
    before = jnp.where(segment == 0, low, pltpu.roll(x, 1, 0))
    out = {0: x}
    for b in range(1, REACH + 1):
        out[b] = pltpu.roll(jnp.where(lane < b, after, x), LANES - b, 1)
        out[-b] = pltpu.roll(jnp.where(lane >= LANES - b, before, x), b, 1)
    return out


def kernel(
    disp_ref, vel_ref, bonds_ref, disp_out, vel_out,
    given, given_bonds, state, far, half, packed, masks, total, bond_rows, edge_out, edges_out,
    rows_in, row_bonds_in, edge_in, rows_next, edges_next, load, send, recv,
):
    rows = disp_ref.shape[1]
    segments = disp_ref.shape[2] // LANES
    groups = rows // GROUP
    assert rows % GROUP == 0 and groups >= 4
    loads = [
        pltpu.make_async_copy(disp_ref, given.at[0:2], load.at[0]),
        pltpu.make_async_copy(vel_ref, given.at[2:4], load.at[1]),
        pltpu.make_async_copy(bonds_ref, given_bonds, load.at[2]),
    ]
    for c in loads:
        c.start()

    gx, gy = lax.axis_index("gx"), lax.axis_index("gy")
    nx, ny = lax.axis_size("gx"), lax.axis_size("gy")
    gx_at = {-1: lax.rem(gx + nx - 1, nx), 0: gx, 1: lax.rem(gx + 1, nx)}
    gy_at = {-1: lax.rem(gy + ny - 1, ny), 0: gy, 1: lax.rem(gy + 1, ny)}
    around = [(x, y) for x in (-1, 0, 1) for y in (-1, 0, 1) if (x, y) != (0, 0)]

    barrier = pltpu.get_barrier_semaphore()
    for x, y in around:
        pl.semaphore_signal(
            barrier, inc=1, device_id=(gx_at[x], gy_at[y]), device_id_type=MESH
        )

    def remote(phase, index, src, dst, x, y):
        return pltpu.make_async_remote_copy(
            src_ref=src, dst_ref=dst, send_sem=send.at[phase, index],
            recv_sem=recv.at[phase, index], device_id=(x, y), device_id_type=MESH,
        )

    def row_copy(phase, side):
        start = pl.ds(side * (rows - REACH), REACH)
        x = lax.rem(gx + nx - 1 + 2 * side, nx)
        if phase is None:
            return remote(0, side, state.at[:, start], rows_in.at[1 - side], x, gy)
        return remote(
            phase, side, half.at[phase - 1, :, start], rows_next.at[phase - 1, 1 - side], x, gy
        )

    def bond_copy():
        return remote(0, 2, bond_rows, row_bonds_in, gx_at[1], gy)

    def edge_copy(phase, side, x):
        slot = 1 - x
        index = 3 + 3 * side + slot
        if phase is None:
            planes = 4 if x < 0 else 8
            return remote(
                0, index, edge_out.at[side, 0:planes], edge_in.at[1 - side, slot, 0:planes],
                gx_at[x], gy_at[2 * side - 1],
            )
        return remote(
            phase, index, edges_out.at[phase - 1, side],
            edges_next.at[phase - 1, 1 - side, slot], gx_at[x], gy_at[2 * side - 1],
        )

    def mid_copies(phase):
        return [edge_copy(phase, side, 0) for side in (0, 1)]

    def rest_copies(phase):
        out = [row_copy(phase, side) for side in (0, 1)]
        if phase is None:
            out.append(bond_copy())
        return out + [edge_copy(phase, side, x) for side in (0, 1) for x in (1, -1)]

    def by_segments(block):
        return block.reshape(rows, segments, LANES)

    last = (segments - 1) * LANES
    loads[0].wait()
    loads[1].wait()
    for plane in range(4):
        block = given[plane]
        state[plane] = by_segments(block)
        edge_out[0, plane] = block[:, 0:LANES]
        edge_out[1, plane] = block[:, last : last + LANES]
    loads[2].wait()
    words = []
    for w in range(4):
        word = given_bonds[w].astype(jnp.float32)
        edge_out[0, 4 + w] = word[:, 0:LANES]
        edge_out[1, 4 + w] = word[:, last : last + LANES]
        words.append(by_segments(word))
    slot = 0
    row_bond_slots = {}
    for a in range(1, REACH + 1):
        for r in range(rows - a, rows):
            bond_rows[slot] = words[a][r]
            row_bond_slots[(a, r - rows)] = slot
            slot += 1
    pl.semaphore_wait(barrier, len(around))
    for c in [row_copy(None, 0), row_copy(None, 1)] + mid_copies(None) + rest_copies(None)[2:]:
        c.start()
    own_packed = words[0] * PACK[0] + words[1] * PACK[1] + words[2] * PACK[2] + words[3] * PACK[3]
    packed[...] = own_packed.astype(jnp.int32)

    segment = lax.broadcasted_iota(jnp.int32, (segments, LANES), 0)
    lane = lax.broadcasted_iota(jnp.int32, (segments, LANES), 1)

    def mask_index(a, b):
        return (a + REACH) * len(SHIFTS) + b + REACH

    def mask(word, bit, a, b):
        return jnp.where(jnp.bitwise_and(word, 1 << bit) != 0, 1.0 / (a * a + b * b), 0.0)

    def push_masks(r, word, low, high):
        for b, value in spread(word, low, high, segment, lane).items():
            for a in range(REACH + 1):
                if in_table(a, -b):
                    masks[mask_index(-a, b), r + REACH + a] = mask(value, bond_bit(a, -b), a, b)

    def edge_word(slot, e):
        out = []
        for side in (0, 1):
            value = edge_in[side, slot, 4, pl.ds(e, 1), :]
            for w in range(1, 4):
                value = value + edge_in[side, slot, 4 + w, pl.ds(e, 1), :] * PACK[w]
            out.append(value.astype(jnp.int32))
        return out

    def place_first(r, rows_of, slot, e):
        for plane in range(4):
            low = edge_in[0, slot, plane, pl.ds(e, 1), :]
            high = edge_in[1, slot, plane, pl.ds(e, 1), :]
            for b, value in spread(rows_of(plane), low, high, segment, lane).items():
                far[plane, b + REACH, r + REACH] = value + float(b) if plane == 1 and b else value

    def place_next(phase, r, rows_of, slot, e):
        for plane in range(2):
            low = edges_next[phase - 1, 0, slot, plane, pl.ds(e, 1), :]
            high = edges_next[phase - 1, 1, slot, plane, pl.ds(e, 1), :]
            for b, value in spread(rows_of(plane), low, high, segment, lane).items():
                far[2 + plane, b + REACH, r + REACH] = value
                far[plane, b + REACH, r + REACH] += TIME_STEP * value

    @pl.loop(0, rows)
    def _(r):
        word = packed[r]
        for a, b in OFFSETS:
            if in_table(a, b):
                masks[mask_index(a, b), r + REACH] = mask(word, bond_bit(a, b), a, b)

    def evaluate(near, top, signed, sums):
        force_x, force_y = sums
        for a, size in signed:
            near_x = near[0] - lax.convert_element_type(a, jnp.float32)
            at = pl.ds(top + REACH + a, GROUP)
            for b in SHIFTS:
                if size == 0 and b == 0:
                    continue
                rest = STIFFNESS * math.sqrt(size * size + b * b + SOFTENING)
                along_x = far[0, b + REACH, at] - near_x
                along_y = far[1, b + REACH, at] - near[1]
                speed_x = far[2, b + REACH, at] - near[2]
                speed_y = far[3, b + REACH, at] - near[3]
                inverse = lax.rsqrt(along_x * along_x + (along_y * along_y + SOFTENING))
                closing = (along_x * speed_x + along_y * speed_y) * inverse
                if DAMPING != 1.0:
                    closing = closing * DAMPING
                tension = masks[mask_index(a, b), pl.ds(top + REACH, GROUP)] * (
                    STIFFNESS - inverse * (rest - closing)
                )
                force_x += tension * along_x
                force_y += tension * along_y
        return force_x, force_y

    def near_of(top):
        return [far[f, REACH, pl.ds(top + REACH, GROUP)] for f in range(4)]

    zero = jnp.zeros((GROUP, segments, LANES), jnp.float32)

    def inner_forces():
        @pl.loop(0, 2)
        def _(side):
            sign = 1 - 2 * side
            for depth, sizes in ((0, range(0, REACH + 1)), (1, range(-2, REACH + 1))):
                top = depth * GROUP + side * (rows - (2 * depth + 1) * GROUP)
                signed = [(sign * a, abs(a)) for a in sizes]
                sums = evaluate(near_of(top), top, signed, (zero, zero))
                for f in range(2):
                    total[f, pl.ds(top, GROUP)] = sums[f]

        if groups > 4:
            @pl.loop(2, groups - 2)
            def _(group):
                top = group * GROUP
                sums = evaluate(near_of(top), top, [(a, abs(a)) for a in SHIFTS], (zero, zero))
                for f in range(2):
                    total[f, pl.ds(top, GROUP)] = sums[f]

    def kicked(phase, top, near, sums):
        again = jnp.where(jnp.logical_and(phase > 0, phase < STEPS), 1.0, 0.0)
        for f in range(2):
            kick = (0.5 * TIME_STEP) * sums[f]
            value = (near[2 + f] + kick) + kick * again
            half[phase, f, pl.ds(top, GROUP)] = value
            for k in range(GROUP):
                edges_out[phase, 0, f, pl.ds(top + k, 1), :] = value[k, 0:1]
                edges_out[phase, 1, f, pl.ds(top + k, 1), :] = value[k, segments - 1 : segments]

    def outer_forces(phase):
        if groups > 4:
            @pl.loop(2, groups - 2)
            def _(group):
                top = group * GROUP
                kicked(phase, top, near_of(top), [total[f, pl.ds(top, GROUP)] for f in range(2)])

        @pl.loop(0, 2)
        def _(side):
            sign = 1 - 2 * side
            for depth, sizes in ((0, (-1, -2, -3)), (1, (-3,))):
                top = depth * GROUP + side * (rows - (2 * depth + 1) * GROUP)
                near = near_of(top)
                sums = [total[f, pl.ds(top, GROUP)] for f in range(2)]
                signed = [(sign * a, abs(a)) for a in sizes]
                kicked(phase, top, near, evaluate(near, top, signed, sums))

            @pl.when(phase < STEPS)
            def _():
                row_copy(phase + 1, side).start()

    @pl.loop(0, STEPS + 1)
    def _(phase):
        @pl.when(phase == 0)
        def _():
            for c in mid_copies(None):
                c.wait_recv()

            @pl.loop(0, rows)
            def _(r):
                place_first(r, lambda plane: state[plane, r], 1, r)
                push_masks(r, packed[r], *edge_word(1, r))

        @pl.when(phase > 0)
        def _():
            for c in mid_copies(phase):
                c.wait_recv()

            @pl.loop(0, groups)
            def _(group):
                for k in range(GROUP):
                    r = group * GROUP + k
                    place_next(phase, r, lambda plane: half[phase - 1, plane, r], 1, r)

        inner_forces()

        @pl.when(phase == 0)
        def _():
            for c in rest_copies(None):
                c.wait_recv()

            @pl.loop(0, REACH)
            def _(k):
                r = k - REACH
                place_first(r, lambda plane: rows_in[0, plane, k], 0, rows - REACH + k)
                place_first(rows + k, lambda plane: rows_in[1, plane, k], 2, k)

            for r in range(-REACH, 0):
                word = jnp.zeros((segments, LANES), jnp.float32)
                for a in range(-r, REACH + 1):
                    word = word + row_bonds_in[row_bond_slots[(a, r)]] * PACK[a]
                push_masks(r, word.astype(jnp.int32), *edge_word(0, rows + r))

        @pl.when(phase > 0)
        def _():
            for c in rest_copies(phase):
                c.wait_recv()

            @pl.loop(0, REACH)
            def _(k):
                place_next(
                    phase, k - REACH, lambda plane: rows_next[phase - 1, 0, plane, k], 0,
                    rows - REACH + k,
                )
                place_next(
                    phase, rows + k, lambda plane: rows_next[phase - 1, 1, plane, k], 2, k
                )

        outer_forces(phase)

        @pl.when(phase < STEPS)
        def _():
            for c in mid_copies(phase + 1) + rest_copies(phase + 1)[2:]:
                c.start()

    for f in range(2):
        disp_out[f] = far[f, REACH, REACH : REACH + rows].reshape(rows, segments * LANES)
        vel_out[f] = half[STEPS, f].reshape(rows, segments * LANES)
    for phase in [None, *range(1, STEPS + 1)]:
        for c in mid_copies(phase) + rest_copies(phase):
            c.wait_send()


def per_device(disp, vel, bonds):
    rows, columns = disp.shape[1:]
    segments = columns // LANES
    padded = rows + 2 * REACH
    vmem = lambda *shape: pltpu.VMEM(shape, jnp.float32)
    bond_slots = REACH * (REACH + 1) // 2
    spec = pl.BlockSpec(memory_space=pltpu.VMEM)
    return pl.pallas_call(
        kernel,
        out_shape=(jax.ShapeDtypeStruct(disp.shape, disp.dtype),) * 2,
        in_specs=[pl.BlockSpec(memory_space=pl.ANY)] * 3,
        out_specs=(spec,) * 2,
        scratch_shapes=[
            vmem(4, rows, columns),
            pltpu.VMEM((4, rows, columns), jnp.int32),
            vmem(4, rows, segments, LANES),
            vmem(4, len(SHIFTS), padded, segments, LANES),
            vmem(STEPS + 1, 2, rows, segments, LANES),
            pltpu.VMEM((rows, segments, LANES), jnp.int32),
            vmem(len(SHIFTS) ** 2, padded, segments, LANES),
            vmem(2, rows, segments, LANES),
            vmem(bond_slots, segments, LANES),
            vmem(2, 8, rows, LANES),
            vmem(STEPS + 1, 2, 2, rows, LANES),
            vmem(2, 4, REACH, segments, LANES),
            vmem(bond_slots, segments, LANES),
            vmem(2, 3, 8, rows, LANES),
            vmem(STEPS, 2, 2, REACH, segments, LANES),
            vmem(STEPS, 2, 3, 2, rows, LANES),
            pltpu.SemaphoreType.DMA((3,)),
            pltpu.SemaphoreType.DMA((STEPS + 1, 9)),
            pltpu.SemaphoreType.DMA((STEPS + 1, 9)),
        ],
        compiler_params=pltpu.CompilerParams(
            collective_id=0, has_side_effects=True, vmem_limit_bytes=56 * 1024 * 1024
        ),
    )(disp, vel, bonds)


def solution(mesh):
    spec = P(None, "gx", "gy")
    return jax.shard_map(
        per_device, mesh=mesh, in_specs=(spec,) * 3, out_specs=(spec,) * 2, check_vma=False
    )
```

```python
import functools
import math

import jax
import jax.numpy as jnp
from jax import lax
from jax.experimental import pallas as pl
from jax.experimental.pallas import tpu as pltpu
from jax.sharding import PartitionSpec as P

STEPS = 2
STIFFNESS = 40.0
DAMPING = 1.0
TIME_STEP = 0.05
SOFTENING = 0.0625
REACH = 3
LANES = 128
GROUP = 2
PACK = (1, 8, 1024, 131072)
PACK_SHIFT = (0, 3, 10, 17)
MESH = pl.DeviceIdType.MESH
SHIFTS = tuple(range(-REACH, REACH + 1))


def bond_bit(a, b):
    return b - 1 if a == 0 else PACK_SHIFT[a] + b + REACH


OFFSETS = [(a, b) for a in SHIFTS for b in SHIFTS if (a, b) != (0, 0)]


def in_table(a, b):
    return a > 0 or (a == 0 and b > 0)


def spread(x, low, high, segment, lane):
    segments = x.shape[0]
    after = jnp.where(segment == segments - 1, high, pltpu.roll(x, segments - 1, 0))
    before = jnp.where(segment == 0, low, pltpu.roll(x, 1, 0))
    out = {0: x}
    for b in range(1, REACH + 1):
        out[b] = pltpu.roll(jnp.where(lane < b, after, x), LANES - b, 1)
        out[-b] = pltpu.roll(jnp.where(lane >= LANES - b, before, x), b, 1)
    return out


def kernel(
    disp_ref, vel_ref, bonds_ref, disp_out, vel_out,
    given, given_bonds, state, far, half, packed, masks, total, bond_rows, edge_out, edges_out,
    corner_out, corners_out, rows_in, row_bonds_in, edge_in, corner_in, rows_next, edges_next,
    corners_next, load, send, recv,
):
    rows = disp_ref.shape[1]
    segments = disp_ref.shape[2] // LANES
    groups = rows // GROUP
    assert rows % GROUP == 0 and groups >= 4
    corner_rows = corner_out.shape[2]
    corner_state = 16
    loads = [
        pltpu.make_async_copy(disp_ref, given.at[0:2], load.at[0]),
        pltpu.make_async_copy(vel_ref, given.at[2:4], load.at[1]),
        pltpu.make_async_copy(bonds_ref, given_bonds, load.at[2]),
    ]
    for c in loads:
        c.start()

    gx, gy = lax.axis_index("gx"), lax.axis_index("gy")
    nx, ny = lax.axis_size("gx"), lax.axis_size("gy")
    gx_at = {-1: lax.rem(gx + nx - 1, nx), 0: gx, 1: lax.rem(gx + 1, nx)}
    gy_at = {-1: lax.rem(gy + ny - 1, ny), 0: gy, 1: lax.rem(gy + 1, ny)}
    around = [(x, y) for x in (-1, 0, 1) for y in (-1, 0, 1) if (x, y) != (0, 0)]

    barrier = pltpu.get_barrier_semaphore()
    for x, y in around:
        pl.semaphore_signal(
            barrier, inc=1, device_id=(gx_at[x], gy_at[y]), device_id_type=MESH
        )

    def remote(phase, index, src, dst, x, y):
        return pltpu.make_async_remote_copy(
            src_ref=src, dst_ref=dst, send_sem=send.at[phase, index],
            recv_sem=recv.at[phase, index], device_id=(x, y), device_id_type=MESH,
        )

    def row_copy(phase, side):
        start = pl.ds(side * (rows - REACH), REACH)
        x = lax.rem(gx + nx - 1 + 2 * side, nx)
        if phase is None:
            return remote(0, side, state.at[:, start], rows_in.at[1 - side], x, gy)
        return remote(
            phase, side, half.at[phase - 1, :, start], rows_next.at[phase - 1, 1 - side], x, gy
        )

    def bond_copy():
        return remote(0, 2, bond_rows, row_bonds_in, gx_at[1], gy)

    def edge_copy(phase, side):
        y = gy_at[2 * side - 1]
        if phase is None:
            return remote(0, 3 + side, edge_out.at[side], edge_in.at[1 - side], gx, y)
        return remote(
            phase, 3 + side, edges_out.at[phase - 1, side], edges_next.at[phase - 1, 1 - side], gx, y
        )

    def corner_copy(phase, along, across, first_rows=0):
        x = lax.rem(gx + nx - 1 + 2 * along, nx)
        y = gy_at[2 * across - 1]
        index = 5 + 2 * along + across
        if phase is None:
            part = pl.ds(0, first_rows)
            return remote(
                0, index, corner_out.at[along, across, part],
                corner_in.at[1 - along, 1 - across, part], x, y,
            )
        return remote(
            phase, index, corners_out.at[phase - 1, along, across],
            corners_next.at[phase - 1, 1 - along, 1 - across], x, y,
        )

    def mid_copies(phase):
        return [edge_copy(phase, side) for side in (0, 1)]

    def rest_copies(phase):
        out = [row_copy(phase, side) for side in (0, 1)]
        if phase is None:
            out.append(bond_copy())
        return out + [
            corner_copy(phase, along, across, (corner_state, corner_rows)[along])
            for along in (0, 1) for across in (0, 1)
        ]

    def by_segments(block):
        return block.reshape(rows, segments, LANES)

    last = (segments - 1) * LANES
    loads[0].wait()
    loads[1].wait()
    for plane in range(4):
        block = given[plane]
        state[plane] = by_segments(block)
        edge_out[0, plane] = block[:, 0:LANES]
        edge_out[1, plane] = block[:, last : last + LANES]
        for along in (0, 1):
            top = along * (rows - REACH)
            at = slice(plane * REACH, (plane + 1) * REACH)
            corner_out[along, 0, at] = block[top : top + REACH, 0:LANES]
            corner_out[along, 1, at] = block[top : top + REACH, last : last + LANES]
    loads[2].wait()
    words = []
    for w in range(4):
        word = given_bonds[w].astype(jnp.float32)
        edge_out[0, 4 + w] = word[:, 0:LANES]
        edge_out[1, 4 + w] = word[:, last : last + LANES]
        words.append(by_segments(word))
    slot = 0
    row_bond_slots = {}
    for a in range(1, REACH + 1):
        for r in range(rows - a, rows):
            bond_rows[slot] = words[a][r]
            for across in (0, 1):
                at = corner_state + slot
                corner_out[1, across, at : at + 1] = edge_out[across, 4 + a, r : r + 1]
            row_bond_slots[(a, r - rows)] = slot
            slot += 1
    pl.semaphore_wait(barrier, len(around))
    for c in rest_copies(None) + mid_copies(None):
        c.start()
    own_packed = words[0] * PACK[0] + words[1] * PACK[1] + words[2] * PACK[2] + words[3] * PACK[3]
    packed[...] = own_packed.astype(jnp.int32)

    segment = lax.broadcasted_iota(jnp.int32, (segments, LANES), 0)
    lane = lax.broadcasted_iota(jnp.int32, (segments, LANES), 1)

    def mask_index(a, b):
        return (a + REACH) * len(SHIFTS) + b + REACH

    def mask(word, bit, a, b):
        return jnp.where(jnp.bitwise_and(word, 1 << bit) != 0, 1.0 / (a * a + b * b), 0.0)

    def push_masks(r, word, low, high):
        for b, value in spread(word, low, high, segment, lane).items():
            for a in range(REACH + 1):
                if in_table(a, -b):
                    masks[mask_index(-a, b), r + REACH + a] = mask(value, bond_bit(a, -b), a, b)

    def place_first(r, rows_of, outer):
        for plane in range(4):
            low, high = outer(0, plane), outer(1, plane)
            for b, value in spread(rows_of(plane), low, high, segment, lane).items():
                far[plane, b + REACH, r + REACH] = value + float(b) if plane == 1 and b else value

    def place_next(r, rows_of, outer):
        for plane in range(2):
            low, high = outer(0, plane), outer(1, plane)
            for b, value in spread(rows_of(plane), low, high, segment, lane).items():
                far[2 + plane, b + REACH, r + REACH] = value
                far[plane, b + REACH, r + REACH] += TIME_STEP * value

    @pl.loop(0, rows)
    def _(r):
        word = packed[r]
        for a, b in OFFSETS:
            if in_table(a, b):
                masks[mask_index(a, b), r + REACH] = mask(word, bond_bit(a, b), a, b)

    def evaluate(near, top, signed, sums):
        force_x, force_y = sums
        for a, size in signed:
            near_x = near[0] - lax.convert_element_type(a, jnp.float32)
            at = pl.ds(top + REACH + a, GROUP)
            for b in SHIFTS:
                if size == 0 and b == 0:
                    continue
                rest = STIFFNESS * math.sqrt(size * size + b * b + SOFTENING)
                along_x = far[0, b + REACH, at] - near_x
                along_y = far[1, b + REACH, at] - near[1]
                speed_x = far[2, b + REACH, at] - near[2]
                speed_y = far[3, b + REACH, at] - near[3]
                inverse = lax.rsqrt(along_x * along_x + (along_y * along_y + SOFTENING))
                closing = (along_x * speed_x + along_y * speed_y) * inverse
                if DAMPING != 1.0:
                    closing = closing * DAMPING
                tension = masks[mask_index(a, b), pl.ds(top + REACH, GROUP)] * (
                    STIFFNESS - inverse * (rest - closing)
                )
                force_x += tension * along_x
                force_y += tension * along_y
        return force_x, force_y

    def near_of(top):
        return [far[f, REACH, pl.ds(top + REACH, GROUP)] for f in range(4)]

    zero = jnp.zeros((GROUP, segments, LANES), jnp.float32)

    def inner_forces():
        @pl.loop(0, 2)
        def _(side):
            sign = 1 - 2 * side
            for depth, sizes in ((0, range(0, REACH + 1)), (1, range(-2, REACH + 1))):
                top = depth * GROUP + side * (rows - (2 * depth + 1) * GROUP)
                signed = [(sign * a, abs(a)) for a in sizes]
                sums = evaluate(near_of(top), top, signed, (zero, zero))
                for f in range(2):
                    total[f, pl.ds(top, GROUP)] = sums[f]

        if groups > 4:
            @pl.loop(2, groups - 2)
            def _(group):
                top = group * GROUP
                sums = evaluate(near_of(top), top, [(a, abs(a)) for a in SHIFTS], (zero, zero))
                for f in range(2):
                    total[f, pl.ds(top, GROUP)] = sums[f]

    def kicked(phase, top, near, sums):
        again = jnp.where(jnp.logical_and(phase > 0, phase < STEPS), 1.0, 0.0)
        for f in range(2):
            kick = (0.5 * TIME_STEP) * sums[f]
            value = (near[2 + f] + kick) + kick * again
            half[phase, f, pl.ds(top, GROUP)] = value
            for k in range(GROUP):
                edges_out[phase, 0, f, pl.ds(top + k, 1), :] = value[k, 0:1]
                edges_out[phase, 1, f, pl.ds(top + k, 1), :] = value[k, segments - 1 : segments]

    def outer_forces(phase):
        if groups > 4:
            @pl.loop(2, groups - 2)
            def _(group):
                top = group * GROUP
                kicked(phase, top, near_of(top), [total[f, pl.ds(top, GROUP)] for f in range(2)])

        @pl.loop(0, 2)
        def _(side):
            sign = 1 - 2 * side
            for depth, sizes in ((0, (-1, -2, -3)), (1, (-3,))):
                top = depth * GROUP + side * (rows - (2 * depth + 1) * GROUP)
                near = near_of(top)
                sums = [total[f, pl.ds(top, GROUP)] for f in range(2)]
                signed = [(sign * a, abs(a)) for a in sizes]
                kicked(phase, top, near, evaluate(near, top, signed, sums))

            @pl.when(phase < STEPS)
            def _():
                row_copy(phase + 1, side).start()
                for f in range(2):
                    for k in range(REACH):
                        r = side * (rows - REACH) + k
                        for across in (0, 1):
                            corners_out[phase, side, across, f * REACH + k : f * REACH + k + 1, :] = (
                                edges_out[phase, across, f, pl.ds(r, 1), :]
                            )
                for across in (0, 1):
                    corner_copy(phase + 1, side, across).start()

    @pl.loop(0, STEPS + 1)
    def _(phase):
        @pl.when(phase == 0)
        def _():
            for c in mid_copies(None):
                c.wait_recv()

            @pl.loop(0, groups)
            def _(group):
                for k in range(GROUP):
                    r = group * GROUP + k
                    place_first(
                        r, lambda plane: state[plane, r],
                        lambda side, plane: edge_in[side, plane, pl.ds(r, 1), :],
                    )
                    outer = []
                    for side in (0, 1):
                        value = edge_in[side, 4, pl.ds(r, 1), :]
                        for w in range(1, 4):
                            value = value + edge_in[side, 4 + w, pl.ds(r, 1), :] * PACK[w]
                        outer.append(value.astype(jnp.int32))
                    push_masks(r, packed[r], *outer)

        @pl.when(phase > 0)
        def _():
            for c in mid_copies(phase):
                c.wait_recv()

            @pl.loop(0, groups // 2)
            def _(group):
                for k in range(2 * GROUP):
                    r = group * (2 * GROUP) + k
                    place_next(
                        r, lambda plane: half[phase - 1, plane, r],
                        lambda side, plane: edges_next[phase - 1, side, plane, pl.ds(r, 1), :],
                    )

        inner_forces()

        @pl.when(phase == 0)
        def _():
            for c in rest_copies(None):
                c.wait_recv()

            for along in (0, 1):
                for k in range(REACH):
                    place_first(
                        along * (rows + REACH) - REACH + k, lambda plane: rows_in[along, plane, k],
                        lambda side, plane: corner_in[
                            along, side, plane * REACH + k : plane * REACH + k + 1, :
                        ],
                    )

            for r in range(-REACH, 0):
                word = jnp.zeros((segments, LANES), jnp.float32)
                outer = [jnp.zeros((1, LANES), jnp.float32) for side in (0, 1)]
                for a in range(-r, REACH + 1):
                    slot = row_bond_slots[(a, r)]
                    at = corner_state + slot
                    word = word + row_bonds_in[slot] * PACK[a]
                    for side in (0, 1):
                        outer[side] += corner_in[0, side, at : at + 1, :] * PACK[a]
                push_masks(r, word.astype(jnp.int32), *[x.astype(jnp.int32) for x in outer])

        @pl.when(phase > 0)
        def _():
            for c in rest_copies(phase):
                c.wait_recv()

            for along in (0, 1):
                for k in range(REACH):
                    place_next(
                        along * (rows + REACH) - REACH + k,
                        lambda plane: rows_next[phase - 1, along, plane, k],
                        lambda side, plane: corners_next[
                            phase - 1, along, side, plane * REACH + k : plane * REACH + k + 1, :
                        ],
                    )

        outer_forces(phase)

        @pl.when(phase < STEPS)
        def _():
            for c in mid_copies(phase + 1):
                c.start()

    for f in range(2):
        disp_out[f] = far[f, REACH, REACH : REACH + rows].reshape(rows, segments * LANES)
        vel_out[f] = half[STEPS, f].reshape(rows, segments * LANES)
    for phase in [None, *range(1, STEPS + 1)]:
        for c in mid_copies(phase) + rest_copies(phase):
            c.wait_send()


def store(disp_ref, vel_ref, disp_out, vel_out, sems):
    copies = [
        pltpu.make_async_copy(disp_ref, disp_out, sems.at[0]),
        pltpu.make_async_copy(vel_ref, vel_out, sems.at[1]),
    ]
    for c in copies:
        c.start()
    for c in copies:
        c.wait()


def per_device(disp, vel, bonds):
    rows, columns = disp.shape[1:]
    segments = columns // LANES
    padded = rows + 2 * REACH
    vmem = lambda *shape: pltpu.VMEM(shape, jnp.float32)
    bond_slots = REACH * (REACH + 1) // 2
    spec = pl.BlockSpec(memory_space=pltpu.VMEM)
    results = (jax.ShapeDtypeStruct(disp.shape, disp.dtype),) * 2
    done = pl.pallas_call(
        kernel,
        out_shape=results,
        in_specs=[pl.BlockSpec(memory_space=pltpu.HBM)] * 3,
        out_specs=(spec,) * 2,
        scratch_shapes=[
            vmem(4, rows, columns),
            pltpu.VMEM((4, rows, columns), jnp.int32),
            vmem(4, rows, segments, LANES),
            vmem(4, len(SHIFTS), padded, segments, LANES),
            vmem(STEPS + 1, 2, rows, segments, LANES),
            pltpu.VMEM((rows, segments, LANES), jnp.int32),
            vmem(len(SHIFTS) ** 2, padded, segments, LANES),
            vmem(2, rows, segments, LANES),
            vmem(bond_slots, segments, LANES),
            vmem(2, 8, rows, LANES),
            vmem(STEPS + 1, 2, 2, rows, LANES),
            vmem(2, 2, 24, LANES),
            vmem(STEPS, 2, 2, 8, LANES),
            vmem(2, 4, REACH, segments, LANES),
            vmem(bond_slots, segments, LANES),
            vmem(2, 8, rows, LANES),
            vmem(2, 2, 24, LANES),
            vmem(STEPS, 2, 2, REACH, segments, LANES),
            vmem(STEPS, 2, 2, rows, LANES),
            vmem(STEPS, 2, 2, 8, LANES),
            pltpu.SemaphoreType.DMA((3,)),
            pltpu.SemaphoreType.DMA((STEPS + 1, 9)),
            pltpu.SemaphoreType.DMA((STEPS + 1, 9)),
        ],
        compiler_params=pltpu.CompilerParams(
            collective_id=0, has_side_effects=True, vmem_limit_bytes=20 * 1024 * 1024
        ),
    )(disp, vel, bonds)
    return pl.pallas_call(
        store,
        out_shape=results,
        in_specs=[spec] * 2,
        out_specs=(pl.BlockSpec(memory_space=pltpu.HBM),) * 2,
        scratch_shapes=[pltpu.SemaphoreType.DMA((2,))],
    )(*done)


def solution(mesh):
    spec = P(None, "gx", "gy")
    return jax.shard_map(
        per_device, mesh=mesh, in_specs=(spec,) * 3, out_specs=(spec,) * 2, check_vma=False
    )
```

```python
import functools
import math

import jax
import jax.numpy as jnp
from jax import lax
from jax.experimental import pallas as pl
from jax.experimental.pallas import tpu as pltpu
from jax.sharding import PartitionSpec as P

STEPS = 2
STIFFNESS = 40.0
DAMPING = 1.0
TIME_STEP = 0.05
SOFTENING = 0.0625
REACH = 3
LANES = 128
GROUP = 2
PACK = (1, 8, 1024, 131072)
PACK_SHIFT = (0, 3, 10, 17)
MESH = pl.DeviceIdType.MESH
SHIFTS = tuple(range(-REACH, REACH + 1))


def bond_bit(a, b):
    return b - 1 if a == 0 else PACK_SHIFT[a] + b + REACH


OFFSETS = [(a, b) for a in SHIFTS for b in SHIFTS if (a, b) != (0, 0)]


def in_table(a, b):
    return a > 0 or (a == 0 and b > 0)


def spread(x, low, high, segment, lane):
    segments = x.shape[0]
    after = jnp.where(segment == segments - 1, high, pltpu.roll(x, segments - 1, 0))
    before = jnp.where(segment == 0, low, pltpu.roll(x, 1, 0))
    out = {0: x}
    for b in range(1, REACH + 1):
        out[b] = pltpu.roll(jnp.where(lane < b, after, x), LANES - b, 1)
        out[-b] = pltpu.roll(jnp.where(lane >= LANES - b, before, x), b, 1)
    return out


def kernel(
    disp_ref, vel_ref, bonds_ref, disp_out, vel_out,
    given, given_bonds, state, far, half, packed, masks, total, bond_rows, edge_out, edges_out,
    corner_out, corners_out, rows_in, row_bonds_in, edge_in, corner_in, rows_next, edges_next,
    corners_next, load, send, recv,
):
    rows = disp_ref.shape[1]
    segments = disp_ref.shape[2] // LANES
    groups = rows // GROUP
    assert rows % GROUP == 0 and groups >= 4
    corner_rows = corner_out.shape[2]
    corner_state = 16
    loads = [
        pltpu.make_async_copy(disp_ref, given.at[0:2], load.at[0]),
        pltpu.make_async_copy(vel_ref, given.at[2:4], load.at[1]),
        pltpu.make_async_copy(bonds_ref, given_bonds, load.at[2]),
    ]
    for c in loads:
        c.start()

    gx, gy = lax.axis_index("gx"), lax.axis_index("gy")
    nx, ny = lax.axis_size("gx"), lax.axis_size("gy")
    gx_at = {-1: lax.rem(gx + nx - 1, nx), 0: gx, 1: lax.rem(gx + 1, nx)}
    gy_at = {-1: lax.rem(gy + ny - 1, ny), 0: gy, 1: lax.rem(gy + 1, ny)}
    around = [(x, y) for x in (-1, 0, 1) for y in (-1, 0, 1) if (x, y) != (0, 0)]

    barrier = pltpu.get_barrier_semaphore()
    for x, y in around:
        pl.semaphore_signal(
            barrier, inc=1, device_id=(gx_at[x], gy_at[y]), device_id_type=MESH
        )

    def remote(phase, index, src, dst, x, y):
        return pltpu.make_async_remote_copy(
            src_ref=src, dst_ref=dst, send_sem=send.at[phase, index],
            recv_sem=recv.at[phase, index], device_id=(x, y), device_id_type=MESH,
        )

    def row_copy(phase, side):
        start = pl.ds(side * (rows - REACH), REACH)
        x = lax.rem(gx + nx - 1 + 2 * side, nx)
        if phase is None:
            return remote(0, side, state.at[:, start], rows_in.at[1 - side], x, gy)
        return remote(
            phase, side, half.at[phase - 1, :, start], rows_next.at[phase - 1, 1 - side], x, gy
        )

    def bond_copy():
        return remote(0, 2, bond_rows, row_bonds_in, gx_at[1], gy)

    def edge_copy(phase, side):
        y = gy_at[2 * side - 1]
        if phase is None:
            return remote(0, 3 + side, edge_out.at[side], edge_in.at[1 - side], gx, y)
        return remote(
            phase, 3 + side, edges_out.at[phase - 1, side], edges_next.at[phase - 1, 1 - side], gx, y
        )

    def corner_copy(phase, along, across, first_rows=0):
        x = lax.rem(gx + nx - 1 + 2 * along, nx)
        y = gy_at[2 * across - 1]
        index = 5 + 2 * along + across
        if phase is None:
            part = pl.ds(0, first_rows)
            return remote(
                0, index, corner_out.at[along, across, part],
                corner_in.at[1 - along, 1 - across, part], x, y,
            )
        return remote(
            phase, index, corners_out.at[phase - 1, along, across],
            corners_next.at[phase - 1, 1 - along, 1 - across], x, y,
        )

    def mid_copies(phase):
        return [edge_copy(phase, side) for side in (0, 1)]

    def rest_copies(phase):
        out = [row_copy(phase, side) for side in (0, 1)]
        if phase is None:
            out.append(bond_copy())
        return out + [
            corner_copy(phase, along, across, (corner_state, corner_rows)[along])
            for along in (0, 1) for across in (0, 1)
        ]

    def by_segments(block):
        return block.reshape(rows, segments, LANES)

    last = (segments - 1) * LANES
    loads[0].wait()
    loads[1].wait()
    for plane in range(4):
        block = given[plane]
        state[plane] = by_segments(block)
        edge_out[0, plane] = block[:, 0:LANES]
        edge_out[1, plane] = block[:, last : last + LANES]
        for along in (0, 1):
            top = along * (rows - REACH)
            at = slice(plane * REACH, (plane + 1) * REACH)
            corner_out[along, 0, at] = block[top : top + REACH, 0:LANES]
            corner_out[along, 1, at] = block[top : top + REACH, last : last + LANES]
    loads[2].wait()
    words = []
    for w in range(4):
        word = given_bonds[w].astype(jnp.float32)
        edge_out[0, 4 + w] = word[:, 0:LANES]
        edge_out[1, 4 + w] = word[:, last : last + LANES]
        words.append(by_segments(word))
    slot = 0
    row_bond_slots = {}
    for a in range(1, REACH + 1):
        for r in range(rows - a, rows):
            bond_rows[slot] = words[a][r]
            for across in (0, 1):
                at = corner_state + slot
                corner_out[1, across, at : at + 1] = edge_out[across, 4 + a, r : r + 1]
            row_bond_slots[(a, r - rows)] = slot
            slot += 1
    pl.semaphore_wait(barrier, len(around))
    for c in rest_copies(None) + mid_copies(None):
        c.start()
    own_packed = words[0] * PACK[0] + words[1] * PACK[1] + words[2] * PACK[2] + words[3] * PACK[3]
    packed[...] = own_packed.astype(jnp.int32)

    segment = lax.broadcasted_iota(jnp.int32, (segments, LANES), 0)
    lane = lax.broadcasted_iota(jnp.int32, (segments, LANES), 1)

    def mask_index(a, b):
        return (a + REACH) * len(SHIFTS) + b + REACH

    def mask(word, bit, a, b):
        return jnp.where(jnp.bitwise_and(word, 1 << bit) != 0, 1.0 / (a * a + b * b), 0.0)

    def push_masks(r, word, low, high):
        for b, value in spread(word, low, high, segment, lane).items():
            for a in range(REACH + 1):
                if in_table(a, -b):
                    masks[mask_index(-a, b), r + REACH + a] = mask(value, bond_bit(a, -b), a, b)

    def place_first(r, rows_of, outer):
        for plane in range(4):
            low, high = outer(0, plane), outer(1, plane)
            for b, value in spread(rows_of(plane), low, high, segment, lane).items():
                far[plane, b + REACH, r + REACH] = value + float(b) if plane == 1 and b else value

    def place_next(r, rows_of, outer):
        for plane in range(2):
            low, high = outer(0, plane), outer(1, plane)
            for b, value in spread(rows_of(plane), low, high, segment, lane).items():
                far[2 + plane, b + REACH, r + REACH] = value
                far[plane, b + REACH, r + REACH] += TIME_STEP * value

    @pl.loop(0, rows)
    def _(r):
        word = packed[r]
        for a, b in OFFSETS:
            if in_table(a, b):
                masks[mask_index(a, b), r + REACH] = mask(word, bond_bit(a, b), a, b)

    def evaluate(near, top, signed, sums):
        force_x, force_y = sums
        for a, size in signed:
            near_x = near[0] - lax.convert_element_type(a, jnp.float32)
            at = pl.ds(top + REACH + a, GROUP)
            for b in SHIFTS:
                if size == 0 and b == 0:
                    continue
                rest = STIFFNESS * math.sqrt(size * size + b * b + SOFTENING)
                along_x = far[0, b + REACH, at] - near_x
                along_y = far[1, b + REACH, at] - near[1]
                speed_x = far[2, b + REACH, at] - near[2]
                speed_y = far[3, b + REACH, at] - near[3]
                inverse = lax.rsqrt(along_x * along_x + (along_y * along_y + SOFTENING))
                closing = (along_x * speed_x + along_y * speed_y) * inverse
                if DAMPING != 1.0:
                    closing = closing * DAMPING
                tension = masks[mask_index(a, b), pl.ds(top + REACH, GROUP)] * (
                    STIFFNESS - inverse * (rest - closing)
                )
                force_x += tension * along_x
                force_y += tension * along_y
        return force_x, force_y

    def near_of(top):
        return [far[f, REACH, pl.ds(top + REACH, GROUP)] for f in range(4)]

    zero = jnp.zeros((GROUP, segments, LANES), jnp.float32)

    def inner_forces():
        @pl.loop(0, 2)
        def _(side):
            sign = 1 - 2 * side
            for depth, sizes in ((0, range(0, REACH + 1)), (1, range(-2, REACH + 1))):
                top = depth * GROUP + side * (rows - (2 * depth + 1) * GROUP)
                signed = [(sign * a, abs(a)) for a in sizes]
                sums = evaluate(near_of(top), top, signed, (zero, zero))
                for f in range(2):
                    total[f, pl.ds(top, GROUP)] = sums[f]

        if groups > 4:
            @pl.loop(2, groups - 2)
            def _(group):
                top = group * GROUP
                sums = evaluate(near_of(top), top, [(a, abs(a)) for a in SHIFTS], (zero, zero))
                for f in range(2):
                    total[f, pl.ds(top, GROUP)] = sums[f]

    def kicked(phase, top, near, sums):
        again = jnp.where(jnp.logical_and(phase > 0, phase < STEPS), 1.0, 0.0)
        for f in range(2):
            kick = (0.5 * TIME_STEP) * sums[f]
            value = (near[2 + f] + kick) + kick * again
            half[phase, f, pl.ds(top, GROUP)] = value
            for k in range(GROUP):
                edges_out[phase, 0, f, pl.ds(top + k, 1), :] = value[k, 0:1]
                edges_out[phase, 1, f, pl.ds(top + k, 1), :] = value[k, segments - 1 : segments]

    def outer_forces(phase):
        if groups > 4:
            @pl.loop(2, groups - 2)
            def _(group):
                top = group * GROUP
                kicked(phase, top, near_of(top), [total[f, pl.ds(top, GROUP)] for f in range(2)])

        @pl.loop(0, 2)
        def _(side):
            sign = 1 - 2 * side
            for depth, sizes in ((0, (-1, -2, -3)), (1, (-3,))):
                top = depth * GROUP + side * (rows - (2 * depth + 1) * GROUP)
                near = near_of(top)
                sums = [total[f, pl.ds(top, GROUP)] for f in range(2)]
                signed = [(sign * a, abs(a)) for a in sizes]
                kicked(phase, top, near, evaluate(near, top, signed, sums))

            @pl.when(phase < STEPS)
            def _():
                row_copy(phase + 1, side).start()
                for f in range(2):
                    for k in range(REACH):
                        r = side * (rows - REACH) + k
                        for across in (0, 1):
                            corners_out[phase, side, across, f * REACH + k : f * REACH + k + 1, :] = (
                                edges_out[phase, across, f, pl.ds(r, 1), :]
                            )
                for across in (0, 1):
                    corner_copy(phase + 1, side, across).start()

    @pl.loop(0, STEPS + 1)
    def _(phase):
        @pl.when(phase == 0)
        def _():
            for c in mid_copies(None):
                c.wait_recv()

            @pl.loop(0, groups)
            def _(group):
                for k in range(GROUP):
                    r = group * GROUP + k
                    place_first(
                        r, lambda plane: state[plane, r],
                        lambda side, plane: edge_in[side, plane, pl.ds(r, 1), :],
                    )
                    outer = []
                    for side in (0, 1):
                        value = edge_in[side, 4, pl.ds(r, 1), :]
                        for w in range(1, 4):
                            value = value + edge_in[side, 4 + w, pl.ds(r, 1), :] * PACK[w]
                        outer.append(value.astype(jnp.int32))
                    push_masks(r, packed[r], *outer)

        @pl.when(phase > 0)
        def _():
            for c in mid_copies(phase):
                c.wait_recv()

            @pl.loop(0, groups // 2)
            def _(group):
                for k in range(2 * GROUP):
                    r = group * (2 * GROUP) + k
                    place_next(
                        r, lambda plane: half[phase - 1, plane, r],
                        lambda side, plane: edges_next[phase - 1, side, plane, pl.ds(r, 1), :],
                    )

        inner_forces()

        @pl.when(phase == 0)
        def _():
            for c in rest_copies(None):
                c.wait_recv()

            for along in (0, 1):
                for k in range(REACH):
                    place_first(
                        along * (rows + REACH) - REACH + k, lambda plane: rows_in[along, plane, k],
                        lambda side, plane: corner_in[
                            along, side, plane * REACH + k : plane * REACH + k + 1, :
                        ],
                    )

            for r in range(-REACH, 0):
                word = jnp.zeros((segments, LANES), jnp.float32)
                outer = [jnp.zeros((1, LANES), jnp.float32) for side in (0, 1)]
                for a in range(-r, REACH + 1):
                    slot = row_bond_slots[(a, r)]
                    at = corner_state + slot
                    word = word + row_bonds_in[slot] * PACK[a]
                    for side in (0, 1):
                        outer[side] += corner_in[0, side, at : at + 1, :] * PACK[a]
                push_masks(r, word.astype(jnp.int32), *[x.astype(jnp.int32) for x in outer])

        @pl.when(phase > 0)
        def _():
            for c in rest_copies(phase):
                c.wait_recv()

            for along in (0, 1):
                for k in range(REACH):
                    place_next(
                        along * (rows + REACH) - REACH + k,
                        lambda plane: rows_next[phase - 1, along, plane, k],
                        lambda side, plane: corners_next[
                            phase - 1, along, side, plane * REACH + k : plane * REACH + k + 1, :
                        ],
                    )

        outer_forces(phase)

        @pl.when(phase < STEPS)
        def _():
            for c in mid_copies(phase + 1):
                c.start()

    for f in range(2):
        disp_out[f] = far[f, REACH, REACH : REACH + rows].reshape(rows, segments * LANES)
        vel_out[f] = half[STEPS, f].reshape(rows, segments * LANES)
    for phase in [None, *range(1, STEPS + 1)]:
        for c in mid_copies(phase) + rest_copies(phase):
            c.wait_send()


def per_device(disp, vel, bonds):
    rows, columns = disp.shape[1:]
    segments = columns // LANES
    padded = rows + 2 * REACH
    vmem = lambda *shape: pltpu.VMEM(shape, jnp.float32)
    bond_slots = REACH * (REACH + 1) // 2
    spec = pl.BlockSpec(memory_space=pltpu.VMEM)
    results = (jax.ShapeDtypeStruct(disp.shape, disp.dtype),) * 2
    return pl.pallas_call(
        kernel,
        out_shape=results,
        in_specs=[pl.BlockSpec(memory_space=pltpu.HBM)] * 3,
        out_specs=(spec,) * 2,
        scratch_shapes=[
            vmem(4, rows, columns),
            pltpu.VMEM((4, rows, columns), jnp.int32),
            vmem(4, rows, segments, LANES),
            vmem(4, len(SHIFTS), padded, segments, LANES),
            vmem(STEPS + 1, 2, rows, segments, LANES),
            pltpu.VMEM((rows, segments, LANES), jnp.int32),
            vmem(len(SHIFTS) ** 2, padded, segments, LANES),
            vmem(2, rows, segments, LANES),
            vmem(bond_slots, segments, LANES),
            vmem(2, 8, rows, LANES),
            vmem(STEPS + 1, 2, 2, rows, LANES),
            vmem(2, 2, 24, LANES),
            vmem(STEPS, 2, 2, 8, LANES),
            vmem(2, 4, REACH, segments, LANES),
            vmem(bond_slots, segments, LANES),
            vmem(2, 8, rows, LANES),
            vmem(2, 2, 24, LANES),
            vmem(STEPS, 2, 2, REACH, segments, LANES),
            vmem(STEPS, 2, 2, rows, LANES),
            vmem(STEPS, 2, 2, 8, LANES),
            pltpu.SemaphoreType.DMA((3,)),
            pltpu.SemaphoreType.DMA((STEPS + 1, 9)),
            pltpu.SemaphoreType.DMA((STEPS + 1, 9)),
        ],
        compiler_params=pltpu.CompilerParams(
            collective_id=0, has_side_effects=True, vmem_limit_bytes=55104 * 1024
        ),
    )(disp, vel, bonds)


def solution(mesh):
    spec = P(None, "gx", "gy")
    return jax.shard_map(
        per_device, mesh=mesh, in_specs=(spec,) * 3, out_specs=(spec,) * 2, check_vma=False
    )
```

```python
import functools
import math

import jax
import jax.numpy as jnp
from jax import lax
from jax.experimental import pallas as pl
from jax.experimental.pallas import tpu as pltpu
from jax.sharding import PartitionSpec as P

STEPS = 2
STIFFNESS = 40.0
DAMPING = 1.0
TIME_STEP = 0.05
SOFTENING = 0.0625
REACH = 3
LANES = 128
GROUP = 2
PACK = (1, 8, 1024, 131072)
PACK_SHIFT = (0, 3, 10, 17)
MESH = pl.DeviceIdType.MESH
SHIFTS = tuple(range(-REACH, REACH + 1))


def bond_bit(a, b):
    return b - 1 if a == 0 else PACK_SHIFT[a] + b + REACH


OFFSETS = [(a, b) for a in SHIFTS for b in SHIFTS if (a, b) != (0, 0)]


def in_table(a, b):
    return a > 0 or (a == 0 and b > 0)


def spread(x, low, high, segment, lane):
    segments = x.shape[0]
    after = jnp.where(segment == segments - 1, high, pltpu.roll(x, segments - 1, 0))
    before = jnp.where(segment == 0, low, pltpu.roll(x, 1, 0))
    out = {0: x}
    for b in range(1, REACH + 1):
        out[b] = pltpu.roll(jnp.where(lane < b, after, x), LANES - b, 1)
        out[-b] = pltpu.roll(jnp.where(lane >= LANES - b, before, x), b, 1)
    return out


def kernel(
    disp_ref, vel_ref, bonds_ref, disp_out, half_out, accel_out,
    given, given_bonds, state, far, half, packed, masks, total, bond_rows, edge_out, edges_out,
    corner_out, corners_out, rows_in, row_bonds_in, edge_in, corner_in, rows_next, edges_next,
    corners_next, load, send, recv,
):
    rows = disp_ref.shape[1]
    segments = disp_ref.shape[2] // LANES
    groups = rows // GROUP
    assert rows % GROUP == 0 and groups >= 4
    corner_rows = corner_out.shape[2]
    corner_state = 16
    loads = [
        pltpu.make_async_copy(disp_ref, given.at[0:2], load.at[0]),
        pltpu.make_async_copy(vel_ref, given.at[2:4], load.at[1]),
        pltpu.make_async_copy(bonds_ref, given_bonds, load.at[2]),
    ]
    for c in loads:
        c.start()

    gx, gy = lax.axis_index("gx"), lax.axis_index("gy")
    nx, ny = lax.axis_size("gx"), lax.axis_size("gy")
    gx_at = {-1: lax.rem(gx + nx - 1, nx), 0: gx, 1: lax.rem(gx + 1, nx)}
    gy_at = {-1: lax.rem(gy + ny - 1, ny), 0: gy, 1: lax.rem(gy + 1, ny)}
    around = [(x, y) for x in (-1, 0, 1) for y in (-1, 0, 1) if (x, y) != (0, 0)]

    barrier = pltpu.get_barrier_semaphore()
    for x, y in around:
        pl.semaphore_signal(
            barrier, inc=1, device_id=(gx_at[x], gy_at[y]), device_id_type=MESH
        )

    def remote(phase, index, src, dst, x, y):
        return pltpu.make_async_remote_copy(
            src_ref=src, dst_ref=dst, send_sem=send.at[phase, index],
            recv_sem=recv.at[phase, index], device_id=(x, y), device_id_type=MESH,
        )

    def row_copy(phase, side):
        start = pl.ds(side * (rows - REACH), REACH)
        x = lax.rem(gx + nx - 1 + 2 * side, nx)
        if phase is None:
            return remote(0, side, state.at[:, start], rows_in.at[1 - side], x, gy)
        return remote(
            phase, side, half.at[phase - 1, :, start], rows_next.at[phase - 1, 1 - side], x, gy
        )

    def bond_copy():
        return remote(0, 2, bond_rows, row_bonds_in, gx_at[1], gy)

    def edge_copy(phase, side):
        y = gy_at[2 * side - 1]
        if phase is None:
            return remote(0, 3 + side, edge_out.at[side], edge_in.at[1 - side], gx, y)
        return remote(
            phase, 3 + side, edges_out.at[phase - 1, side], edges_next.at[phase - 1, 1 - side], gx, y
        )

    def corner_copy(phase, along, across, first_rows=0):
        x = lax.rem(gx + nx - 1 + 2 * along, nx)
        y = gy_at[2 * across - 1]
        index = 5 + 2 * along + across
        if phase is None:
            part = pl.ds(0, first_rows)
            return remote(
                0, index, corner_out.at[along, across, part],
                corner_in.at[1 - along, 1 - across, part], x, y,
            )
        return remote(
            phase, index, corners_out.at[phase - 1, along, across],
            corners_next.at[phase - 1, 1 - along, 1 - across], x, y,
        )

    def mid_copies(phase):
        return [edge_copy(phase, side) for side in (0, 1)]

    def rest_copies(phase):
        out = [row_copy(phase, side) for side in (0, 1)]
        if phase is None:
            out.append(bond_copy())
        return out + [
            corner_copy(phase, along, across, (corner_state, corner_rows)[along])
            for along in (0, 1) for across in (0, 1)
        ]

    def by_segments(block):
        return block.reshape(rows, segments, LANES)

    last = (segments - 1) * LANES
    loads[0].wait()
    loads[1].wait()
    for plane in range(4):
        block = given[plane]
        state[plane] = by_segments(block)
        edge_out[0, plane] = block[:, 0:LANES]
        edge_out[1, plane] = block[:, last : last + LANES]
        for along in (0, 1):
            top = along * (rows - REACH)
            at = slice(plane * REACH, (plane + 1) * REACH)
            corner_out[along, 0, at] = block[top : top + REACH, 0:LANES]
            corner_out[along, 1, at] = block[top : top + REACH, last : last + LANES]
    loads[2].wait()
    words = []
    for w in range(4):
        word = given_bonds[w].astype(jnp.float32)
        edge_out[0, 4 + w] = word[:, 0:LANES]
        edge_out[1, 4 + w] = word[:, last : last + LANES]
        words.append(by_segments(word))
    slot = 0
    row_bond_slots = {}
    for a in range(1, REACH + 1):
        for r in range(rows - a, rows):
            bond_rows[slot] = words[a][r]
            for across in (0, 1):
                at = corner_state + slot
                corner_out[1, across, at : at + 1] = edge_out[across, 4 + a, r : r + 1]
            row_bond_slots[(a, r - rows)] = slot
            slot += 1
    pl.semaphore_wait(barrier, len(around))
    for c in rest_copies(None) + mid_copies(None):
        c.start()
    own_packed = words[0] * PACK[0] + words[1] * PACK[1] + words[2] * PACK[2] + words[3] * PACK[3]
    packed[...] = own_packed.astype(jnp.int32)

    segment = lax.broadcasted_iota(jnp.int32, (segments, LANES), 0)
    lane = lax.broadcasted_iota(jnp.int32, (segments, LANES), 1)

    def mask_index(a, b):
        return (a + REACH) * len(SHIFTS) + b + REACH

    def mask(word, bit, a, b):
        return jnp.where(jnp.bitwise_and(word, 1 << bit) != 0, 1.0 / (a * a + b * b), 0.0)

    def push_masks(r, word, low, high):
        for b, value in spread(word, low, high, segment, lane).items():
            for a in range(REACH + 1):
                if in_table(a, -b):
                    masks[mask_index(-a, b), r + REACH + a] = mask(value, bond_bit(a, -b), a, b)

    def place_first(r, rows_of, outer):
        for plane in range(4):
            low, high = outer(0, plane), outer(1, plane)
            for b, value in spread(rows_of(plane), low, high, segment, lane).items():
                far[plane, b + REACH, r + REACH] = value + float(b) if plane == 1 and b else value

    def place_next(r, rows_of, outer):
        for plane in range(2):
            low, high = outer(0, plane), outer(1, plane)
            for b, value in spread(rows_of(plane), low, high, segment, lane).items():
                far[2 + plane, b + REACH, r + REACH] = value
                far[plane, b + REACH, r + REACH] += TIME_STEP * value

    @pl.loop(0, rows)
    def _(r):
        word = packed[r]
        for a, b in OFFSETS:
            if in_table(a, b):
                masks[mask_index(a, b), r + REACH] = mask(word, bond_bit(a, b), a, b)

    def evaluate(near, top, signed, sums):
        force_x, force_y = sums
        for a, size in signed:
            near_x = near[0] - lax.convert_element_type(a, jnp.float32)
            at = pl.ds(top + REACH + a, GROUP)
            for b in SHIFTS:
                if size == 0 and b == 0:
                    continue
                rest = STIFFNESS * math.sqrt(size * size + b * b + SOFTENING)
                along_x = far[0, b + REACH, at] - near_x
                along_y = far[1, b + REACH, at] - near[1]
                speed_x = far[2, b + REACH, at] - near[2]
                speed_y = far[3, b + REACH, at] - near[3]
                inverse = lax.rsqrt(along_x * along_x + (along_y * along_y + SOFTENING))
                closing = (along_x * speed_x + along_y * speed_y) * inverse
                if DAMPING != 1.0:
                    closing = closing * DAMPING
                tension = masks[mask_index(a, b), pl.ds(top + REACH, GROUP)] * (
                    STIFFNESS - inverse * (rest - closing)
                )
                force_x += tension * along_x
                force_y += tension * along_y
        return force_x, force_y

    def near_of(top):
        return [far[f, REACH, pl.ds(top + REACH, GROUP)] for f in range(4)]

    zero = jnp.zeros((GROUP, segments, LANES), jnp.float32)

    def inner_forces():
        @pl.loop(0, 2)
        def _(side):
            sign = 1 - 2 * side
            for depth, sizes in ((0, range(0, REACH + 1)), (1, range(-2, REACH + 1))):
                top = depth * GROUP + side * (rows - (2 * depth + 1) * GROUP)
                signed = [(sign * a, abs(a)) for a in sizes]
                sums = evaluate(near_of(top), top, signed, (zero, zero))
                for f in range(2):
                    total[f, pl.ds(top, GROUP)] = sums[f]

        if groups > 4:
            @pl.loop(2, groups - 2)
            def _(group):
                top = group * GROUP
                sums = evaluate(near_of(top), top, [(a, abs(a)) for a in SHIFTS], (zero, zero))
                for f in range(2):
                    total[f, pl.ds(top, GROUP)] = sums[f]

    def kicked(phase, top, near, sums):
        again = jnp.where(jnp.logical_and(phase > 0, phase < STEPS), 1.0, 0.0)
        for f in range(2):
            kick = (0.5 * TIME_STEP) * sums[f]
            value = (near[2 + f] + kick) + kick * again
            half[phase, f, pl.ds(top, GROUP)] = value
            total[f, pl.ds(top, GROUP)] = sums[f]
            for k in range(GROUP):
                edges_out[phase, 0, f, pl.ds(top + k, 1), :] = value[k, 0:1]
                edges_out[phase, 1, f, pl.ds(top + k, 1), :] = value[k, segments - 1 : segments]

    def outer_forces(phase):
        if groups > 4:
            @pl.loop(2, groups - 2)
            def _(group):
                top = group * GROUP
                kicked(phase, top, near_of(top), [total[f, pl.ds(top, GROUP)] for f in range(2)])

        @pl.loop(0, 2)
        def _(side):
            sign = 1 - 2 * side
            for depth, sizes in ((0, (-1, -2, -3)), (1, (-3,))):
                top = depth * GROUP + side * (rows - (2 * depth + 1) * GROUP)
                near = near_of(top)
                sums = [total[f, pl.ds(top, GROUP)] for f in range(2)]
                signed = [(sign * a, abs(a)) for a in sizes]
                kicked(phase, top, near, evaluate(near, top, signed, sums))

            @pl.when(phase < STEPS)
            def _():
                row_copy(phase + 1, side).start()
                for f in range(2):
                    for k in range(REACH):
                        r = side * (rows - REACH) + k
                        for across in (0, 1):
                            corners_out[phase, side, across, f * REACH + k : f * REACH + k + 1, :] = (
                                edges_out[phase, across, f, pl.ds(r, 1), :]
                            )
                for across in (0, 1):
                    corner_copy(phase + 1, side, across).start()

    @pl.loop(0, STEPS + 1)
    def _(phase):
        @pl.when(phase == 0)
        def _():
            for c in mid_copies(None):
                c.wait_recv()

            @pl.loop(0, groups)
            def _(group):
                for k in range(GROUP):
                    r = group * GROUP + k
                    place_first(
                        r, lambda plane: state[plane, r],
                        lambda side, plane: edge_in[side, plane, pl.ds(r, 1), :],
                    )
                    outer = []
                    for side in (0, 1):
                        value = edge_in[side, 4, pl.ds(r, 1), :]
                        for w in range(1, 4):
                            value = value + edge_in[side, 4 + w, pl.ds(r, 1), :] * PACK[w]
                        outer.append(value.astype(jnp.int32))
                    push_masks(r, packed[r], *outer)

        @pl.when(phase == STEPS)
        def _():
            for f in range(2):
                disp_out[f] = far[f, REACH, REACH : REACH + rows].reshape(rows, segments * LANES)
                half_out[f] = half[STEPS - 1, f].reshape(rows, segments * LANES)

        @pl.when(phase > 0)
        def _():
            for c in mid_copies(phase):
                c.wait_recv()

            @pl.loop(0, groups // 2)
            def _(group):
                for k in range(2 * GROUP):
                    r = group * (2 * GROUP) + k
                    place_next(
                        r, lambda plane: half[phase - 1, plane, r],
                        lambda side, plane: edges_next[phase - 1, side, plane, pl.ds(r, 1), :],
                    )

        inner_forces()

        @pl.when(phase == 0)
        def _():
            for c in rest_copies(None):
                c.wait_recv()

            for along in (0, 1):
                for k in range(REACH):
                    place_first(
                        along * (rows + REACH) - REACH + k, lambda plane: rows_in[along, plane, k],
                        lambda side, plane: corner_in[
                            along, side, plane * REACH + k : plane * REACH + k + 1, :
                        ],
                    )

            for r in range(-REACH, 0):
                word = jnp.zeros((segments, LANES), jnp.float32)
                outer = [jnp.zeros((1, LANES), jnp.float32) for side in (0, 1)]
                for a in range(-r, REACH + 1):
                    slot = row_bond_slots[(a, r)]
                    at = corner_state + slot
                    word = word + row_bonds_in[slot] * PACK[a]
                    for side in (0, 1):
                        outer[side] += corner_in[0, side, at : at + 1, :] * PACK[a]
                push_masks(r, word.astype(jnp.int32), *[x.astype(jnp.int32) for x in outer])

        @pl.when(phase > 0)
        def _():
            for c in rest_copies(phase):
                c.wait_recv()

            for along in (0, 1):
                for k in range(REACH):
                    place_next(
                        along * (rows + REACH) - REACH + k,
                        lambda plane: rows_next[phase - 1, along, plane, k],
                        lambda side, plane: corners_next[
                            phase - 1, along, side, plane * REACH + k : plane * REACH + k + 1, :
                        ],
                    )

        outer_forces(phase)

        @pl.when(phase < STEPS)
        def _():
            for c in mid_copies(phase + 1):
                c.start()

    for f in range(2):
        accel_out[f] = total[f].reshape(rows, segments * LANES)
    for phase in [None, *range(1, STEPS + 1)]:
        for c in mid_copies(phase) + rest_copies(phase):
            c.wait_send()


def per_device(disp, vel, bonds):
    rows, columns = disp.shape[1:]
    segments = columns // LANES
    padded = rows + 2 * REACH
    vmem = lambda *shape: pltpu.VMEM(shape, jnp.float32)
    bond_slots = REACH * (REACH + 1) // 2
    spec = pl.BlockSpec(memory_space=pltpu.VMEM)
    earlier, half, accel = pl.pallas_call(
        kernel,
        out_shape=(jax.ShapeDtypeStruct(disp.shape, disp.dtype),) * 3,
        in_specs=[pl.BlockSpec(memory_space=pltpu.HBM)] * 3,
        out_specs=(spec,) * 3,
        scratch_shapes=[
            vmem(4, rows, columns),
            pltpu.VMEM((4, rows, columns), jnp.int32),
            vmem(4, rows, segments, LANES),
            vmem(4, len(SHIFTS), padded, segments, LANES),
            vmem(STEPS + 1, 2, rows, segments, LANES),
            pltpu.VMEM((rows, segments, LANES), jnp.int32),
            vmem(len(SHIFTS) ** 2, padded, segments, LANES),
            vmem(2, rows, segments, LANES),
            vmem(bond_slots, segments, LANES),
            vmem(2, 8, rows, LANES),
            vmem(STEPS + 1, 2, 2, rows, LANES),
            vmem(2, 2, 24, LANES),
            vmem(STEPS, 2, 2, 8, LANES),
            vmem(2, 4, REACH, segments, LANES),
            vmem(bond_slots, segments, LANES),
            vmem(2, 8, rows, LANES),
            vmem(2, 2, 24, LANES),
            vmem(STEPS, 2, 2, REACH, segments, LANES),
            vmem(STEPS, 2, 2, rows, LANES),
            vmem(STEPS, 2, 2, 8, LANES),
            pltpu.SemaphoreType.DMA((3,)),
            pltpu.SemaphoreType.DMA((STEPS + 1, 9)),
            pltpu.SemaphoreType.DMA((STEPS + 1, 9)),
        ],
        compiler_params=pltpu.CompilerParams(
            collective_id=0, has_side_effects=True, vmem_limit_bytes=55040 * 1024
        ),
    )(disp, vel, bonds)
    return earlier + TIME_STEP * half, half + 0.5 * TIME_STEP * accel


def solution(mesh):
    spec = P(None, "gx", "gy")
    return jax.shard_map(
        per_device, mesh=mesh, in_specs=(spec,) * 3, out_specs=(spec,) * 2, check_vma=False
    )
```

```python
import functools
import math

import jax
import jax.numpy as jnp
from jax import lax
from jax.experimental import pallas as pl
from jax.experimental.pallas import tpu as pltpu
from jax.sharding import PartitionSpec as P

STEPS = 2
STIFFNESS = 40.0
DAMPING = 1.0
TIME_STEP = 0.05
SOFTENING = 0.0625
REACH = 3
LANES = 128
GROUP = 2
PACK = (1, 8, 1024, 131072)
PACK_SHIFT = (0, 3, 10, 17)
MESH = pl.DeviceIdType.MESH
SHIFTS = tuple(range(-REACH, REACH + 1))


def bond_bit(a, b):
    return b - 1 if a == 0 else PACK_SHIFT[a] + b + REACH


OFFSETS = [(a, b) for a in SHIFTS for b in SHIFTS if (a, b) != (0, 0)]


def in_table(a, b):
    return a > 0 or (a == 0 and b > 0)


def spread(x, low, high, segment, lane):
    segments = x.shape[0]
    after = jnp.where(segment == segments - 1, high, pltpu.roll(x, segments - 1, 0))
    before = jnp.where(segment == 0, low, pltpu.roll(x, 1, 0))
    out = {0: x}
    for b in range(1, REACH + 1):
        out[b] = pltpu.roll(jnp.where(lane < b, after, x), LANES - b, 1)
        out[-b] = pltpu.roll(jnp.where(lane >= LANES - b, before, x), b, 1)
    return out


def kernel(
    disp_ref, vel_ref, bonds_ref, disp_out, half_out, accel_out,
    given, given_bonds, state, far, half, packed, masks, total, bond_rows, edge_out, edges_out,
    corner_out, corners_out, rows_in, row_bonds_in, edge_in, corner_in, rows_next, edges_next,
    corners_next, load, send, recv,
):
    rows = disp_ref.shape[1]
    segments = disp_ref.shape[2] // LANES
    groups = rows // GROUP
    assert rows % GROUP == 0 and groups >= 4
    corner_state = 16
    loads = [
        pltpu.make_async_copy(disp_ref, given.at[0:2], load.at[0]),
        pltpu.make_async_copy(vel_ref, given.at[2:4], load.at[1]),
        pltpu.make_async_copy(bonds_ref, given_bonds, load.at[2]),
    ]
    for c in loads:
        c.start()

    gx, gy = lax.axis_index("gx"), lax.axis_index("gy")
    nx, ny = lax.axis_size("gx"), lax.axis_size("gy")
    gx_at = {-1: lax.rem(gx + nx - 1, nx), 0: gx, 1: lax.rem(gx + 1, nx)}
    gy_at = {-1: lax.rem(gy + ny - 1, ny), 0: gy, 1: lax.rem(gy + 1, ny)}
    around = [(x, y) for x in (-1, 0, 1) for y in (-1, 0, 1) if (x, y) != (0, 0)]

    barrier = pltpu.get_barrier_semaphore()
    for x, y in around:
        pl.semaphore_signal(
            barrier, inc=1, device_id=(gx_at[x], gy_at[y]), device_id_type=MESH
        )

    def remote(phase, index, src, dst, x, y):
        return pltpu.make_async_remote_copy(
            src_ref=src, dst_ref=dst, send_sem=send.at[phase, index],
            recv_sem=recv.at[phase, index], device_id=(x, y), device_id_type=MESH,
        )

    def row_copy(phase, side):
        start = pl.ds(side * (rows - REACH), REACH)
        x = lax.rem(gx + nx - 1 + 2 * side, nx)
        if phase is None:
            return remote(0, side, state.at[:, start], rows_in.at[1 - side], x, gy)
        return remote(
            phase, side, half.at[phase - 1, :, start], rows_next.at[phase - 1, 1 - side], x, gy
        )

    def bond_copy():
        return remote(0, 2, bond_rows, row_bonds_in, gx_at[1], gy)

    def edge_copy(phase, side):
        y = gy_at[2 * side - 1]
        if phase is None:
            return remote(0, 3 + side, edge_out.at[side], edge_in.at[1 - side], gx, y)
        return remote(
            phase, 3 + side, edges_out.at[phase - 1, side], edges_next.at[phase - 1, 1 - side], gx, y
        )

    def corner_copy(phase, along, across):
        x = lax.rem(gx + nx - 1 + 2 * along, nx)
        y = gy_at[2 * across - 1]
        index = 5 + 2 * along + across
        if phase is None:
            return remote(
                0, index, corner_out.at[along, across], corner_in.at[1 - along, 1 - across], x, y
            )
        return remote(
            phase, index, corners_out.at[phase - 1, along, across],
            corners_next.at[phase - 1, 1 - along, 1 - across], x, y,
        )

    def mid_copies(phase):
        return [edge_copy(phase, side) for side in (0, 1)]

    def rest_copies(phase):
        out = [row_copy(phase, side) for side in (0, 1)]
        if phase is None:
            out.append(bond_copy())
        return out + [
            corner_copy(phase, along, across) for along in (0, 1) for across in (0, 1)
        ]

    def by_segments(block):
        return block.reshape(rows, segments, LANES)

    last = (segments - 1) * LANES
    loads[0].wait()
    loads[1].wait()
    for plane in range(4):
        block = given[plane]
        state[plane] = by_segments(block)
        edge_out[0, plane] = block[:, 0:LANES]
        edge_out[1, plane] = block[:, last : last + LANES]
        for along in (0, 1):
            top = along * (rows - REACH)
            at = slice(plane * REACH, (plane + 1) * REACH)
            corner_out[along, 0, at] = block[top : top + REACH, 0:LANES]
            corner_out[along, 1, at] = block[top : top + REACH, last : last + LANES]
    loads[2].wait()
    words = []
    for w in range(4):
        word = given_bonds[w].astype(jnp.float32)
        edge_out[0, 4 + w] = word[:, 0:LANES]
        edge_out[1, 4 + w] = word[:, last : last + LANES]
        words.append(by_segments(word))
    slot = 0
    row_bond_slots = {}
    for a in range(1, REACH + 1):
        for r in range(rows - a, rows):
            bond_rows[slot] = words[a][r]
            for across in (0, 1):
                at = corner_state + slot
                corner_out[1, across, at : at + 1] = edge_out[across, 4 + a, r : r + 1]
            row_bond_slots[(a, r - rows)] = slot
            slot += 1
    pl.semaphore_wait(barrier, len(around))
    for c in rest_copies(None) + mid_copies(None):
        c.start()
    own_packed = words[0] * PACK[0] + words[1] * PACK[1] + words[2] * PACK[2] + words[3] * PACK[3]
    packed[...] = own_packed.astype(jnp.int32)

    segment = lax.broadcasted_iota(jnp.int32, (segments, LANES), 0)
    lane = lax.broadcasted_iota(jnp.int32, (segments, LANES), 1)

    def mask_index(a, b):
        return (a + REACH) * len(SHIFTS) + b + REACH

    def mask(word, bit, a, b):
        return jnp.where(jnp.bitwise_and(word, 1 << bit) != 0, 1.0 / (a * a + b * b), 0.0)

    def push_masks(r, word, low, high):
        for b, value in spread(word, low, high, segment, lane).items():
            for a in range(REACH + 1):
                if in_table(a, -b):
                    masks[mask_index(-a, b), r + REACH + a] = mask(value, bond_bit(a, -b), a, b)

    def place_first(r, rows_of, outer):
        for plane in range(4):
            low, high = outer(0, plane), outer(1, plane)
            for b, value in spread(rows_of(plane), low, high, segment, lane).items():
                far[plane, b + REACH, r + REACH] = value + float(b) if plane == 1 and b else value

    def place_next(r, rows_of, outer):
        for plane in range(2):
            low, high = outer(0, plane), outer(1, plane)
            for b, value in spread(rows_of(plane), low, high, segment, lane).items():
                far[2 + plane, b + REACH, r + REACH] = value
                far[plane, b + REACH, r + REACH] += TIME_STEP * value

    @pl.loop(0, rows)
    def _(r):
        word = packed[r]
        for a, b in OFFSETS:
            if in_table(a, b):
                masks[mask_index(a, b), r + REACH] = mask(word, bond_bit(a, b), a, b)

    def evaluate(near, top, signed, sums):
        force_x, force_y = sums
        for a, size in signed:
            near_x = near[0] - lax.convert_element_type(a, jnp.float32)
            at = pl.ds(top + REACH + a, GROUP)
            for b in SHIFTS:
                if size == 0 and b == 0:
                    continue
                rest = STIFFNESS * math.sqrt(size * size + b * b + SOFTENING)
                along_x = far[0, b + REACH, at] - near_x
                along_y = far[1, b + REACH, at] - near[1]
                speed_x = far[2, b + REACH, at] - near[2]
                speed_y = far[3, b + REACH, at] - near[3]
                inverse = lax.rsqrt(along_x * along_x + (along_y * along_y + SOFTENING))
                closing = (along_x * speed_x + along_y * speed_y) * inverse
                if DAMPING != 1.0:
                    closing = closing * DAMPING
                tension = masks[mask_index(a, b), pl.ds(top + REACH, GROUP)] * (
                    STIFFNESS - inverse * (rest - closing)
                )
                force_x += tension * along_x
                force_y += tension * along_y
        return force_x, force_y

    def near_of(top):
        return [far[f, REACH, pl.ds(top + REACH, GROUP)] for f in range(4)]

    zero = jnp.zeros((GROUP, segments, LANES), jnp.float32)

    def inner_forces():
        @pl.loop(0, 2)
        def _(side):
            sign = 1 - 2 * side
            for depth, sizes in ((0, range(0, REACH + 1)), (1, range(-2, REACH + 1))):
                top = depth * GROUP + side * (rows - (2 * depth + 1) * GROUP)
                signed = [(sign * a, abs(a)) for a in sizes]
                sums = evaluate(near_of(top), top, signed, (zero, zero))
                for f in range(2):
                    total[f, pl.ds(top, GROUP)] = sums[f]

        if groups > 4:
            @pl.loop(2, groups - 2)
            def _(group):
                top = group * GROUP
                sums = evaluate(near_of(top), top, [(a, abs(a)) for a in SHIFTS], (zero, zero))
                for f in range(2):
                    total[f, pl.ds(top, GROUP)] = sums[f]

    def kicked(phase, top, near, sums):
        again = jnp.where(jnp.logical_and(phase > 0, phase < STEPS), 1.0, 0.0)
        for f in range(2):
            kick = (0.5 * TIME_STEP) * sums[f]
            value = (near[2 + f] + kick) + kick * again
            half[phase, f, pl.ds(top, GROUP)] = value
            total[f, pl.ds(top, GROUP)] = sums[f]
            for k in range(GROUP):
                edges_out[phase, 0, f, pl.ds(top + k, 1), :] = value[k, 0:1]
                edges_out[phase, 1, f, pl.ds(top + k, 1), :] = value[k, segments - 1 : segments]

    def outer_forces(phase):
        if groups > 4:
            @pl.loop(2, groups - 2)
            def _(group):
                top = group * GROUP
                kicked(phase, top, near_of(top), [total[f, pl.ds(top, GROUP)] for f in range(2)])

        @pl.loop(0, 2)
        def _(side):
            @pl.when(phase == 0)
            def _():
                row_copy(None, 1 - side).wait_recv()
                for across in (0, 1):
                    corner_copy(None, 1 - side, across).wait_recv()
                for k in range(REACH):
                    place_first(
                        side * (rows + REACH) - REACH + k, lambda plane: rows_in[side, plane, k],
                        lambda across, plane: corner_in[
                            side, across, plane * REACH + k : plane * REACH + k + 1, :
                        ],
                    )

            @pl.when(jnp.logical_and(phase == 0, side == 0))
            def _():
                bond_copy().wait_recv()
                for r in range(-REACH, 0):
                    word = jnp.zeros((segments, LANES), jnp.float32)
                    outer = [jnp.zeros((1, LANES), jnp.float32) for across in (0, 1)]
                    for a in range(-r, REACH + 1):
                        slot = row_bond_slots[(a, r)]
                        at = corner_state + slot
                        word = word + row_bonds_in[slot] * PACK[a]
                        for across in (0, 1):
                            outer[across] += corner_in[0, across, at : at + 1, :] * PACK[a]
                    push_masks(r, word.astype(jnp.int32), *[x.astype(jnp.int32) for x in outer])

            @pl.when(phase > 0)
            def _():
                row_copy(phase, 1 - side).wait_recv()
                for across in (0, 1):
                    corner_copy(phase, 1 - side, across).wait_recv()
                for k in range(REACH):
                    place_next(
                        side * (rows + REACH) - REACH + k,
                        lambda plane: rows_next[phase - 1, side, plane, k],
                        lambda across, plane: corners_next[
                            phase - 1, side, across, plane * REACH + k : plane * REACH + k + 1, :
                        ],
                    )

            sign = 1 - 2 * side
            for depth, sizes in ((0, (-1, -2, -3)), (1, (-3,))):
                top = depth * GROUP + side * (rows - (2 * depth + 1) * GROUP)
                near = near_of(top)
                sums = [total[f, pl.ds(top, GROUP)] for f in range(2)]
                signed = [(sign * a, abs(a)) for a in sizes]
                kicked(phase, top, near, evaluate(near, top, signed, sums))

            @pl.when(phase < STEPS)
            def _():
                row_copy(phase + 1, side).start()
                for f in range(2):
                    for k in range(REACH):
                        r = side * (rows - REACH) + k
                        for across in (0, 1):
                            corners_out[phase, side, across, f * REACH + k : f * REACH + k + 1, :] = (
                                edges_out[phase, across, f, pl.ds(r, 1), :]
                            )
                for across in (0, 1):
                    corner_copy(phase + 1, side, across).start()

    @pl.loop(0, STEPS + 1)
    def _(phase):
        @pl.when(phase == 0)
        def _():
            for c in mid_copies(None):
                c.wait_recv()

            @pl.loop(0, groups)
            def _(group):
                for k in range(GROUP):
                    r = group * GROUP + k
                    place_first(
                        r, lambda plane: state[plane, r],
                        lambda side, plane: edge_in[side, plane, pl.ds(r, 1), :],
                    )
                    outer = []
                    for side in (0, 1):
                        value = edge_in[side, 4, pl.ds(r, 1), :]
                        for w in range(1, 4):
                            value = value + edge_in[side, 4 + w, pl.ds(r, 1), :] * PACK[w]
                        outer.append(value.astype(jnp.int32))
                    push_masks(r, packed[r], *outer)

        @pl.when(phase == STEPS)
        def _():
            for f in range(2):
                disp_out[f] = far[f, REACH, REACH : REACH + rows].reshape(rows, segments * LANES)
                half_out[f] = half[STEPS - 1, f].reshape(rows, segments * LANES)

        @pl.when(phase > 0)
        def _():
            for c in mid_copies(phase):
                c.wait_recv()

            @pl.loop(0, groups // 2)
            def _(group):
                for k in range(2 * GROUP):
                    r = group * (2 * GROUP) + k
                    place_next(
                        r, lambda plane: half[phase - 1, plane, r],
                        lambda side, plane: edges_next[phase - 1, side, plane, pl.ds(r, 1), :],
                    )

        inner_forces()

        outer_forces(phase)

        @pl.when(phase < STEPS)
        def _():
            for c in mid_copies(phase + 1):
                c.start()

    for f in range(2):
        accel_out[f] = total[f].reshape(rows, segments * LANES)
    for phase in [None, *range(1, STEPS + 1)]:
        for c in mid_copies(phase) + rest_copies(phase):
            c.wait_send()


def per_device(disp, vel, bonds):
    rows, columns = disp.shape[1:]
    segments = columns // LANES
    padded = rows + 2 * REACH
    vmem = lambda *shape: pltpu.VMEM(shape, jnp.float32)
    bond_slots = REACH * (REACH + 1) // 2
    spec = pl.BlockSpec(memory_space=pltpu.VMEM)
    earlier, half, accel = pl.pallas_call(
        kernel,
        out_shape=(jax.ShapeDtypeStruct(disp.shape, disp.dtype),) * 3,
        in_specs=[pl.BlockSpec(memory_space=pltpu.HBM)] * 3,
        out_specs=(spec,) * 3,
        scratch_shapes=[
            vmem(4, rows, columns),
            pltpu.VMEM((4, rows, columns), jnp.int32),
            vmem(4, rows, segments, LANES),
            vmem(4, len(SHIFTS), padded, segments, LANES),
            vmem(STEPS + 1, 2, rows, segments, LANES),
            pltpu.VMEM((rows, segments, LANES), jnp.int32),
            vmem(len(SHIFTS) ** 2, padded, segments, LANES),
            vmem(2, rows, segments, LANES),
            vmem(bond_slots, segments, LANES),
            vmem(2, 8, rows, LANES),
            vmem(STEPS + 1, 2, 2, rows, LANES),
            vmem(2, 2, 24, LANES),
            vmem(STEPS, 2, 2, 8, LANES),
            vmem(2, 4, REACH, segments, LANES),
            vmem(bond_slots, segments, LANES),
            vmem(2, 8, rows, LANES),
            vmem(2, 2, 24, LANES),
            vmem(STEPS, 2, 2, REACH, segments, LANES),
            vmem(STEPS, 2, 2, rows, LANES),
            vmem(STEPS, 2, 2, 8, LANES),
            pltpu.SemaphoreType.DMA((3,)),
            pltpu.SemaphoreType.DMA((STEPS + 1, 9)),
            pltpu.SemaphoreType.DMA((STEPS + 1, 9)),
        ],
        compiler_params=pltpu.CompilerParams(
            collective_id=0, has_side_effects=True, vmem_limit_bytes=55040 * 1024
        ),
    )(disp, vel, bonds)
    return earlier + TIME_STEP * half, half + 0.5 * TIME_STEP * accel


def solution(mesh):
    spec = P(None, "gx", "gy")
    return jax.shard_map(
        per_device, mesh=mesh, in_specs=(spec,) * 3, out_specs=(spec,) * 2, check_vma=False
    )
```

```python
import functools
import math

import jax
import jax.numpy as jnp
from jax import lax
from jax.experimental import pallas as pl
from jax.experimental.pallas import tpu as pltpu
from jax.sharding import PartitionSpec as P

STEPS = 2
STIFFNESS = 40.0
DAMPING = 1.0
TIME_STEP = 0.05
SOFTENING = 0.0625
REACH = 3
LANES = 128
GROUP = 2
PACK = (1, 8, 1024, 131072)
PACK_SHIFT = (0, 3, 10, 17)
MESH = pl.DeviceIdType.MESH
SHIFTS = tuple(range(-REACH, REACH + 1))


def bond_bit(a, b):
    return b - 1 if a == 0 else PACK_SHIFT[a] + b + REACH


OFFSETS = [(a, b) for a in SHIFTS for b in SHIFTS if (a, b) != (0, 0)]


def in_table(a, b):
    return a > 0 or (a == 0 and b > 0)


def spread(x, low, high, segment, lane):
    segments = x.shape[0]
    after = jnp.where(segment == segments - 1, high, pltpu.roll(x, segments - 1, 0))
    before = jnp.where(segment == 0, low, pltpu.roll(x, 1, 0))
    out = {0: x}
    for b in range(1, REACH + 1):
        out[b] = pltpu.roll(jnp.where(lane < b, after, x), LANES - b, 1)
        out[-b] = pltpu.roll(jnp.where(lane >= LANES - b, before, x), b, 1)
    return out


def kernel(
    disp_ref, vel_ref, bonds_ref, disp_out, half_out, accel_out,
    given, given_bonds, state, far, half, packed, masks, total, bond_rows, edge_out, edges_out,
    corner_out, corners_out, rows_in, row_bonds_in, edge_in, corner_in, rows_next, edges_next,
    corners_next, load, send, recv,
):
    rows = disp_ref.shape[1]
    segments = disp_ref.shape[2] // LANES
    groups = rows // GROUP
    assert rows % GROUP == 0 and groups >= 4
    corner_rows = corner_out.shape[2]
    corner_state = 16
    loads = [
        pltpu.make_async_copy(disp_ref, given.at[0:2], load.at[0]),
        pltpu.make_async_copy(vel_ref, given.at[2:4], load.at[1]),
        pltpu.make_async_copy(bonds_ref, given_bonds, load.at[2]),
    ]
    for c in loads:
        c.start()

    gx, gy = lax.axis_index("gx"), lax.axis_index("gy")
    nx, ny = lax.axis_size("gx"), lax.axis_size("gy")
    gx_at = {-1: lax.rem(gx + nx - 1, nx), 0: gx, 1: lax.rem(gx + 1, nx)}
    gy_at = {-1: lax.rem(gy + ny - 1, ny), 0: gy, 1: lax.rem(gy + 1, ny)}
    around = [(x, y) for x in (-1, 0, 1) for y in (-1, 0, 1) if (x, y) != (0, 0)]

    barrier = pltpu.get_barrier_semaphore()
    for x, y in around:
        pl.semaphore_signal(
            barrier, inc=1, device_id=(gx_at[x], gy_at[y]), device_id_type=MESH
        )

    def remote(phase, index, src, dst, x, y):
        return pltpu.make_async_remote_copy(
            src_ref=src, dst_ref=dst, send_sem=send.at[phase, index],
            recv_sem=recv.at[phase, index], device_id=(x, y), device_id_type=MESH,
        )

    def row_copy(phase, side):
        start = pl.ds(side * (rows - REACH), REACH)
        x = lax.rem(gx + nx - 1 + 2 * side, nx)
        if phase is None:
            return remote(0, side, state.at[:, start], rows_in.at[1 - side], x, gy)
        return remote(
            phase, side, half.at[phase - 1, :, start], rows_next.at[phase - 1, 1 - side], x, gy
        )

    def bond_copy():
        return remote(0, 2, bond_rows, row_bonds_in, gx_at[1], gy)

    def edge_copy(phase, side):
        y = gy_at[2 * side - 1]
        if phase is None:
            return remote(0, 3 + side, edge_out.at[side], edge_in.at[1 - side], gx, y)
        return remote(
            phase, 3 + side, edges_out.at[phase - 1, side], edges_next.at[phase - 1, 1 - side], gx, y
        )

    def corner_copy(phase, along, across, first_rows=0):
        x = lax.rem(gx + nx - 1 + 2 * along, nx)
        y = gy_at[2 * across - 1]
        index = 5 + 2 * along + across
        if phase is None:
            part = pl.ds(0, first_rows)
            return remote(
                0, index, corner_out.at[along, across, part],
                corner_in.at[1 - along, 1 - across, part], x, y,
            )
        return remote(
            phase, index, corners_out.at[phase - 1, along, across],
            corners_next.at[phase - 1, 1 - along, 1 - across], x, y,
        )

    def mid_copies(phase):
        return [edge_copy(phase, side) for side in (0, 1)]

    def rest_copies(phase):
        out = [row_copy(phase, side) for side in (0, 1)]
        if phase is None:
            out.append(bond_copy())
        return out + [
            corner_copy(phase, along, across, (corner_state, corner_rows)[along])
            for along in (0, 1) for across in (0, 1)
        ]

    def by_segments(block):
        return block.reshape(rows, segments, LANES)

    last = (segments - 1) * LANES
    loads[0].wait()
    loads[1].wait()
    for plane in range(4):
        block = given[plane]
        state[plane] = by_segments(block)
        edge_out[0, plane] = block[:, 0:LANES]
        edge_out[1, plane] = block[:, last : last + LANES]
        for along in (0, 1):
            top = along * (rows - REACH)
            at = slice(plane * REACH, (plane + 1) * REACH)
            corner_out[along, 0, at] = block[top : top + REACH, 0:LANES]
            corner_out[along, 1, at] = block[top : top + REACH, last : last + LANES]
    loads[2].wait()
    words = []
    for w in range(4):
        word = given_bonds[w].astype(jnp.float32)
        edge_out[0, 4 + w] = word[:, 0:LANES]
        edge_out[1, 4 + w] = word[:, last : last + LANES]
        words.append(by_segments(word))
    slot = 0
    row_bond_slots = {}
    for a in range(1, REACH + 1):
        for r in range(rows - a, rows):
            bond_rows[slot] = words[a][r]
            for across in (0, 1):
                at = corner_state + slot
                corner_out[1, across, at : at + 1] = edge_out[across, 4 + a, r : r + 1]
            row_bond_slots[(a, r - rows)] = slot
            slot += 1
    pl.semaphore_wait(barrier, len(around))
    for c in mid_copies(None) + rest_copies(None):
        c.start()
    own_packed = words[0] * PACK[0] + words[1] * PACK[1] + words[2] * PACK[2] + words[3] * PACK[3]
    packed[...] = own_packed.astype(jnp.int32)

    segment = lax.broadcasted_iota(jnp.int32, (segments, LANES), 0)
    lane = lax.broadcasted_iota(jnp.int32, (segments, LANES), 1)

    def mask_index(a, b):
        return (a + REACH) * len(SHIFTS) + b + REACH

    def mask(word, bit, a, b):
        return jnp.where(jnp.bitwise_and(word, 1 << bit) != 0, 1.0 / (a * a + b * b), 0.0)

    def push_masks(r, word, low, high):
        for b, value in spread(word, low, high, segment, lane).items():
            for a in range(REACH + 1):
                if in_table(a, -b):
                    masks[mask_index(-a, b), r + REACH + a] = mask(value, bond_bit(a, -b), a, b)

    def place_first(r, rows_of, outer):
        for plane in range(4):
            low, high = outer(0, plane), outer(1, plane)
            for b, value in spread(rows_of(plane), low, high, segment, lane).items():
                far[plane, b + REACH, r + REACH] = value + float(b) if plane == 1 and b else value

    def place_next(r, rows_of, outer):
        for plane in range(2):
            low, high = outer(0, plane), outer(1, plane)
            for b, value in spread(rows_of(plane), low, high, segment, lane).items():
                far[2 + plane, b + REACH, r + REACH] = value
                far[plane, b + REACH, r + REACH] += TIME_STEP * value

    @pl.loop(0, rows)
    def _(r):
        word = packed[r]
        for a, b in OFFSETS:
            if in_table(a, b):
                masks[mask_index(a, b), r + REACH] = mask(word, bond_bit(a, b), a, b)

    def evaluate(near, top, signed, sums):
        force_x, force_y = sums
        for a, size in signed:
            near_x = near[0] - lax.convert_element_type(a, jnp.float32)
            at = pl.ds(top + REACH + a, GROUP)
            for b in SHIFTS:
                if size == 0 and b == 0:
                    continue
                rest = STIFFNESS * math.sqrt(size * size + b * b + SOFTENING)
                along_x = far[0, b + REACH, at] - near_x
                along_y = far[1, b + REACH, at] - near[1]
                speed_x = far[2, b + REACH, at] - near[2]
                speed_y = far[3, b + REACH, at] - near[3]
                inverse = lax.rsqrt(along_x * along_x + (along_y * along_y + SOFTENING))
                closing = (along_x * speed_x + along_y * speed_y) * inverse
                if DAMPING != 1.0:
                    closing = closing * DAMPING
                tension = masks[mask_index(a, b), pl.ds(top + REACH, GROUP)] * (
                    STIFFNESS - inverse * (rest - closing)
                )
                force_x += tension * along_x
                force_y += tension * along_y
        return force_x, force_y

    def near_of(top):
        return [far[f, REACH, pl.ds(top + REACH, GROUP)] for f in range(4)]

    zero = jnp.zeros((GROUP, segments, LANES), jnp.float32)

    def inner_forces():
        @pl.loop(0, 2)
        def _(side):
            sign = 1 - 2 * side
            for depth, sizes in ((0, range(0, REACH + 1)), (1, range(-2, REACH + 1))):
                top = depth * GROUP + side * (rows - (2 * depth + 1) * GROUP)
                signed = [(sign * a, abs(a)) for a in sizes]
                sums = evaluate(near_of(top), top, signed, (zero, zero))
                for f in range(2):
                    total[f, pl.ds(top, GROUP)] = sums[f]

        if groups > 4:
            @pl.loop(2, groups - 2)
            def _(group):
                top = group * GROUP
                sums = evaluate(near_of(top), top, [(a, abs(a)) for a in SHIFTS], (zero, zero))
                for f in range(2):
                    total[f, pl.ds(top, GROUP)] = sums[f]

    def kicked(phase, top, near, sums):
        again = jnp.where(jnp.logical_and(phase > 0, phase < STEPS), 1.0, 0.0)
        for f in range(2):
            kick = (0.5 * TIME_STEP) * sums[f]
            value = (near[2 + f] + kick) + kick * again
            half[phase, f, pl.ds(top, GROUP)] = value
            total[f, pl.ds(top, GROUP)] = sums[f]
            for k in range(GROUP):
                edges_out[phase, 0, f, pl.ds(top + k, 1), :] = value[k, 0:1]
                edges_out[phase, 1, f, pl.ds(top + k, 1), :] = value[k, segments - 1 : segments]

    def outer_forces(phase):
        if groups > 4:
            @pl.loop(2, groups - 2)
            def _(group):
                top = group * GROUP
                kicked(phase, top, near_of(top), [total[f, pl.ds(top, GROUP)] for f in range(2)])

        @pl.loop(0, 2)
        def _(side):
            sign = 1 - 2 * side
            for depth, sizes in ((0, (-1, -2, -3)), (1, (-3,))):
                top = depth * GROUP + side * (rows - (2 * depth + 1) * GROUP)
                near = near_of(top)
                sums = [total[f, pl.ds(top, GROUP)] for f in range(2)]
                signed = [(sign * a, abs(a)) for a in sizes]
                kicked(phase, top, near, evaluate(near, top, signed, sums))

    @pl.loop(0, STEPS + 1)
    def _(phase):
        @pl.when(phase == 0)
        def _():
            for c in mid_copies(None):
                c.wait_recv()

            @pl.loop(0, groups // 2)
            def _(group):
                for k in range(2 * GROUP):
                    r = group * (2 * GROUP) + k
                    place_first(
                        r, lambda plane: state[plane, r],
                        lambda side, plane: edge_in[side, plane, pl.ds(r, 1), :],
                    )
                    outer = []
                    for side in (0, 1):
                        value = edge_in[side, 4, pl.ds(r, 1), :]
                        for w in range(1, 4):
                            value = value + edge_in[side, 4 + w, pl.ds(r, 1), :] * PACK[w]
                        outer.append(value.astype(jnp.int32))
                    push_masks(r, packed[r], *outer)

        @pl.when(phase == STEPS)
        def _():
            for f in range(2):
                disp_out[f] = far[f, REACH, REACH : REACH + rows].reshape(rows, segments * LANES)
                half_out[f] = half[STEPS - 1, f].reshape(rows, segments * LANES)

        @pl.when(phase > 0)
        def _():
            for c in mid_copies(phase):
                c.wait_recv()

            for r in range(rows):
                place_next(
                    r, lambda plane: half[phase - 1, plane, r],
                    lambda side, plane: edges_next[phase - 1, side, plane, r : r + 1, :],
                )

        inner_forces()

        @pl.when(phase == 0)
        def _():
            for c in rest_copies(None):
                c.wait_recv()

            for along in (0, 1):
                for k in range(REACH):
                    place_first(
                        along * (rows + REACH) - REACH + k, lambda plane: rows_in[along, plane, k],
                        lambda side, plane: corner_in[
                            along, side, plane * REACH + k : plane * REACH + k + 1, :
                        ],
                    )

            for r in range(-REACH, 0):
                word = jnp.zeros((segments, LANES), jnp.float32)
                outer = [jnp.zeros((1, LANES), jnp.float32) for side in (0, 1)]
                for a in range(-r, REACH + 1):
                    slot = row_bond_slots[(a, r)]
                    at = corner_state + slot
                    word = word + row_bonds_in[slot] * PACK[a]
                    for side in (0, 1):
                        outer[side] += corner_in[0, side, at : at + 1, :] * PACK[a]
                push_masks(r, word.astype(jnp.int32), *[x.astype(jnp.int32) for x in outer])

        @pl.when(phase > 0)
        def _():
            for c in rest_copies(phase):
                c.wait_recv()

            for along in (0, 1):
                for k in range(REACH):
                    place_next(
                        along * (rows + REACH) - REACH + k,
                        lambda plane: rows_next[phase - 1, along, plane, k],
                        lambda side, plane: corners_next[
                            phase - 1, along, side, plane * REACH + k : plane * REACH + k + 1, :
                        ],
                    )

        outer_forces(phase)

        @pl.when(phase < STEPS)
        def _():
            for c in mid_copies(phase + 1) + [row_copy(phase + 1, side) for side in (0, 1)]:
                c.start()
            for along in (0, 1):
                for across in (0, 1):
                    for f in range(2):
                        r = along * (rows - REACH)
                        corners_out[phase, along, across, f * REACH : (f + 1) * REACH, :] = (
                            edges_out[phase, across, f, r : r + REACH, :]
                        )
                    corner_copy(phase + 1, along, across).start()

    for f in range(2):
        accel_out[f] = total[f].reshape(rows, segments * LANES)
    for phase in [None, *range(1, STEPS + 1)]:
        for c in mid_copies(phase) + rest_copies(phase):
            c.wait_send()


def per_device(disp, vel, bonds):
    rows, columns = disp.shape[1:]
    segments = columns // LANES
    padded = rows + 2 * REACH
    vmem = lambda *shape: pltpu.VMEM(shape, jnp.float32)
    bond_slots = REACH * (REACH + 1) // 2
    spec = pl.BlockSpec(memory_space=pltpu.VMEM)
    earlier, half, accel = pl.pallas_call(
        kernel,
        out_shape=(jax.ShapeDtypeStruct(disp.shape, disp.dtype),) * 3,
        in_specs=[pl.BlockSpec(memory_space=pltpu.HBM)] * 3,
        out_specs=(spec,) * 3,
        scratch_shapes=[
            vmem(4, rows, columns),
            pltpu.VMEM((4, rows, columns), jnp.int32),
            vmem(4, rows, segments, LANES),
            vmem(4, len(SHIFTS), padded, segments, LANES),
            vmem(STEPS + 1, 2, rows, segments, LANES),
            pltpu.VMEM((rows, segments, LANES), jnp.int32),
            vmem(len(SHIFTS) ** 2, padded, segments, LANES),
            vmem(2, rows, segments, LANES),
            vmem(bond_slots, segments, LANES),
            vmem(2, 8, rows, LANES),
            vmem(STEPS + 1, 2, 2, rows, LANES),
            vmem(2, 2, 24, LANES),
            vmem(STEPS, 2, 2, 8, LANES),
            vmem(2, 4, REACH, segments, LANES),
            vmem(bond_slots, segments, LANES),
            vmem(2, 8, rows, LANES),
            vmem(2, 2, 24, LANES),
            vmem(STEPS, 2, 2, REACH, segments, LANES),
            vmem(STEPS, 2, 2, rows, LANES),
            vmem(STEPS, 2, 2, 8, LANES),
            pltpu.SemaphoreType.DMA((3,)),
            pltpu.SemaphoreType.DMA((STEPS + 1, 9)),
            pltpu.SemaphoreType.DMA((STEPS + 1, 9)),
        ],
        compiler_params=pltpu.CompilerParams(
            collective_id=0, has_side_effects=True, vmem_limit_bytes=55040 * 1024
        ),
    )(disp, vel, bonds)
    return earlier + TIME_STEP * half, half + 0.5 * TIME_STEP * accel


def solution(mesh):
    spec = P(None, "gx", "gy")
    return jax.shard_map(
        per_device, mesh=mesh, in_specs=(spec,) * 3, out_specs=(spec,) * 2, check_vma=False
    )
```

```python
import functools
import math

import jax
import jax.numpy as jnp
from jax import lax
from jax.experimental import pallas as pl
from jax.experimental.pallas import tpu as pltpu
from jax.sharding import PartitionSpec as P

STEPS = 2
STIFFNESS = 40.0
DAMPING = 1.0
TIME_STEP = 0.05
SOFTENING = 0.0625
REACH = 3
LANES = 128
GROUP = 2
PACK = (1, 8, 1024, 131072)
PACK_SHIFT = (0, 3, 10, 17)
MESH = pl.DeviceIdType.MESH
SHIFTS = tuple(range(-REACH, REACH + 1))


def bond_bit(a, b):
    return b - 1 if a == 0 else PACK_SHIFT[a] + b + REACH


OFFSETS = [(a, b) for a in SHIFTS for b in SHIFTS if (a, b) != (0, 0)]


def in_table(a, b):
    return a > 0 or (a == 0 and b > 0)


def spread(x, low, high, segment, lane):
    segments = x.shape[0]
    after = jnp.where(segment == segments - 1, high, pltpu.roll(x, segments - 1, 0))
    before = jnp.where(segment == 0, low, pltpu.roll(x, 1, 0))
    out = {0: x}
    for b in range(1, REACH + 1):
        out[b] = pltpu.roll(jnp.where(lane < b, after, x), LANES - b, 1)
        out[-b] = pltpu.roll(jnp.where(lane >= LANES - b, before, x), b, 1)
    return out


def kernel(
    disp_ref, vel_ref, bonds_ref, disp_out, half_out, accel_out,
    given, given_bonds, state, far, half, packed, masks, total, bond_rows, edge_out, edges_out,
    corner_out, corners_out, rows_in, row_bonds_in, edge_in, corner_in, rows_next, edges_next,
    corners_next, load, send, recv,
):
    rows = disp_ref.shape[1]
    segments = disp_ref.shape[2] // LANES
    groups = rows // GROUP
    assert rows % GROUP == 0 and groups >= 4
    corner_rows = corner_out.shape[2]
    corner_state = 16
    loads = [
        pltpu.make_async_copy(disp_ref, given.at[0:2], load.at[0]),
        pltpu.make_async_copy(vel_ref, given.at[2:4], load.at[1]),
        pltpu.make_async_copy(bonds_ref, given_bonds, load.at[2]),
    ]
    for c in loads:
        c.start()

    gx, gy = lax.axis_index("gx"), lax.axis_index("gy")
    nx, ny = lax.axis_size("gx"), lax.axis_size("gy")
    gx_at = {-1: lax.rem(gx + nx - 1, nx), 0: gx, 1: lax.rem(gx + 1, nx)}
    gy_at = {-1: lax.rem(gy + ny - 1, ny), 0: gy, 1: lax.rem(gy + 1, ny)}
    around = [(x, y) for x in (-1, 0, 1) for y in (-1, 0, 1) if (x, y) != (0, 0)]

    barrier = pltpu.get_barrier_semaphore()
    for x, y in around:
        pl.semaphore_signal(
            barrier, inc=1, device_id=(gx_at[x], gy_at[y]), device_id_type=MESH
        )

    def remote(phase, index, src, dst, x, y):
        return pltpu.make_async_remote_copy(
            src_ref=src, dst_ref=dst, send_sem=send.at[phase, index],
            recv_sem=recv.at[phase, index], device_id=(x, y), device_id_type=MESH,
        )

    def row_copy(phase, side):
        start = pl.ds(side * (rows - REACH), REACH)
        x = lax.rem(gx + nx - 1 + 2 * side, nx)
        if phase is None:
            return remote(0, side, state.at[:, start], rows_in.at[1 - side], x, gy)
        return remote(
            phase, side, half.at[phase - 1, :, start], rows_next.at[phase - 1, 1 - side], x, gy
        )

    def bond_copy():
        return remote(0, 2, bond_rows, row_bonds_in, gx_at[1], gy)

    def edge_copy(phase, side):
        y = gy_at[2 * side - 1]
        if phase is None:
            return remote(0, 3 + side, edge_out.at[side], edge_in.at[1 - side], gx, y)
        return remote(
            phase, 3 + side, edges_out.at[phase - 1, side], edges_next.at[phase - 1, 1 - side], gx, y
        )

    def corner_copy(phase, along, across, first_rows=0):
        x = lax.rem(gx + nx - 1 + 2 * along, nx)
        y = gy_at[2 * across - 1]
        index = 5 + 2 * along + across
        if phase is None:
            part = pl.ds(0, first_rows)
            return remote(
                0, index, corner_out.at[along, across, part],
                corner_in.at[1 - along, 1 - across, part], x, y,
            )
        return remote(
            phase, index, corners_out.at[phase - 1, along, across],
            corners_next.at[phase - 1, 1 - along, 1 - across], x, y,
        )

    def mid_copies(phase):
        return [edge_copy(phase, side) for side in (0, 1)]

    def rest_copies(phase):
        out = [row_copy(phase, side) for side in (0, 1)]
        if phase is None:
            out.append(bond_copy())
        return out + [
            corner_copy(phase, along, across, (corner_state, corner_rows)[along])
            for along in (0, 1) for across in (0, 1)
        ]

    def by_segments(block):
        return block.reshape(rows, segments, LANES)

    last = (segments - 1) * LANES
    loads[0].wait()
    loads[1].wait()
    for plane in range(4):
        block = given[plane]
        state[plane] = by_segments(block)
        edge_out[0, plane] = block[:, 0:LANES]
        edge_out[1, plane] = block[:, last : last + LANES]
        for along in (0, 1):
            top = along * (rows - REACH)
            at = slice(plane * REACH, (plane + 1) * REACH)
            corner_out[along, 0, at] = block[top : top + REACH, 0:LANES]
            corner_out[along, 1, at] = block[top : top + REACH, last : last + LANES]
    loads[2].wait()
    words = []
    for w in range(4):
        word = given_bonds[w].astype(jnp.float32)
        edge_out[0, 4 + w] = word[:, 0:LANES]
        edge_out[1, 4 + w] = word[:, last : last + LANES]
        words.append(by_segments(word))
    slot = 0
    row_bond_slots = {}
    for a in range(1, REACH + 1):
        for r in range(rows - a, rows):
            bond_rows[slot] = words[a][r]
            for across in (0, 1):
                at = corner_state + slot
                corner_out[1, across, at : at + 1] = edge_out[across, 4 + a, r : r + 1]
            row_bond_slots[(a, r - rows)] = slot
            slot += 1
    pl.semaphore_wait(barrier, len(around))
    for c in mid_copies(None) + rest_copies(None):
        c.start()
    own_packed = words[0] * PACK[0] + words[1] * PACK[1] + words[2] * PACK[2] + words[3] * PACK[3]
    packed[...] = own_packed.astype(jnp.int32)

    segment = lax.broadcasted_iota(jnp.int32, (segments, LANES), 0)
    lane = lax.broadcasted_iota(jnp.int32, (segments, LANES), 1)

    def mask_index(a, b):
        return (a + REACH) * len(SHIFTS) + b + REACH

    def mask(word, bit, a, b):
        return jnp.where(jnp.bitwise_and(word, 1 << bit) != 0, 1.0 / (a * a + b * b), 0.0)

    def push_masks(r, word, low, high):
        for b, value in spread(word, low, high, segment, lane).items():
            for a in range(REACH + 1):
                if in_table(a, -b):
                    masks[mask_index(-a, b), r + REACH + a] = mask(value, bond_bit(a, -b), a, b)

    def place_first(r, rows_of, outer):
        for plane in range(4):
            low, high = outer(0, plane), outer(1, plane)
            for b, value in spread(rows_of(plane), low, high, segment, lane).items():
                far[plane, b + REACH, r + REACH] = value + float(b) if plane == 1 and b else value

    def place_next(r, rows_of, outer):
        for plane in range(2):
            low, high = outer(0, plane), outer(1, plane)
            for b, value in spread(rows_of(plane), low, high, segment, lane).items():
                far[2 + plane, b + REACH, r + REACH] = value
                far[plane, b + REACH, r + REACH] += TIME_STEP * value

    @pl.loop(0, rows)
    def _(r):
        word = packed[r]
        for a, b in OFFSETS:
            if in_table(a, b):
                masks[mask_index(a, b), r + REACH] = mask(word, bond_bit(a, b), a, b)

    def evaluate(near, top, signed, sums):
        force_x, force_y = sums
        for a, size in signed:
            near_x = near[0] - float(a)
            at = pl.ds(top + REACH + a, GROUP)
            for b in SHIFTS:
                if size == 0 and b == 0:
                    continue
                rest = STIFFNESS * math.sqrt(size * size + b * b + SOFTENING)
                along_x = far[0, b + REACH, at] - near_x
                along_y = far[1, b + REACH, at] - near[1]
                speed_x = far[2, b + REACH, at] - near[2]
                speed_y = far[3, b + REACH, at] - near[3]
                inverse = lax.rsqrt(along_x * along_x + (along_y * along_y + SOFTENING))
                closing = (along_x * speed_x + along_y * speed_y) * inverse
                if DAMPING != 1.0:
                    closing = closing * DAMPING
                tension = masks[mask_index(a, b), pl.ds(top + REACH, GROUP)] * (
                    STIFFNESS - inverse * (rest - closing)
                )
                force_x += tension * along_x
                force_y += tension * along_y
        return force_x, force_y

    def near_of(top):
        return [far[f, REACH, pl.ds(top + REACH, GROUP)] for f in range(4)]

    zero = jnp.zeros((GROUP, segments, LANES), jnp.float32)

    def inner_forces():
        for side in (0, 1):
            sign = 1 - 2 * side
            for depth, sizes in ((0, range(0, REACH + 1)), (1, range(-2, REACH + 1))):
                top = depth * GROUP + side * (rows - (2 * depth + 1) * GROUP)
                signed = [(sign * a, abs(a)) for a in sizes]
                sums = evaluate(near_of(top), top, signed, (zero, zero))
                for f in range(2):
                    total[f, pl.ds(top, GROUP)] = sums[f]

        if groups > 4:
            @pl.loop(2, groups - 2)
            def _(group):
                top = group * GROUP
                sums = evaluate(near_of(top), top, [(a, abs(a)) for a in SHIFTS], (zero, zero))
                for f in range(2):
                    total[f, pl.ds(top, GROUP)] = sums[f]

    def kicked(phase, top, near, sums):
        again = jnp.where(jnp.logical_and(phase > 0, phase < STEPS), 1.0, 0.0)
        for f in range(2):
            kick = (0.5 * TIME_STEP) * sums[f]
            value = (near[2 + f] + kick) + kick * again
            half[phase, f, pl.ds(top, GROUP)] = value
            total[f, pl.ds(top, GROUP)] = sums[f]
            for k in range(GROUP):
                edges_out[phase, 0, f, pl.ds(top + k, 1), :] = value[k, 0:1]
                edges_out[phase, 1, f, pl.ds(top + k, 1), :] = value[k, segments - 1 : segments]

    def outer_forces(phase):
        if groups > 4:
            @pl.loop(2, groups - 2)
            def _(group):
                top = group * GROUP
                kicked(phase, top, near_of(top), [total[f, pl.ds(top, GROUP)] for f in range(2)])

        for side in (0, 1):
            sign = 1 - 2 * side
            for depth, sizes in ((0, (-1, -2, -3)), (1, (-3,))):
                top = depth * GROUP + side * (rows - (2 * depth + 1) * GROUP)
                near = near_of(top)
                sums = [total[f, pl.ds(top, GROUP)] for f in range(2)]
                signed = [(sign * a, abs(a)) for a in sizes]
                kicked(phase, top, near, evaluate(near, top, signed, sums))

    @pl.loop(0, STEPS + 1)
    def _(phase):
        @pl.when(phase == 0)
        def _():
            for c in mid_copies(None):
                c.wait_recv()

            @pl.loop(0, groups // 2)
            def _(group):
                for k in range(2 * GROUP):
                    r = group * (2 * GROUP) + k
                    place_first(
                        r, lambda plane: state[plane, r],
                        lambda side, plane: edge_in[side, plane, pl.ds(r, 1), :],
                    )
                    outer = []
                    for side in (0, 1):
                        value = edge_in[side, 4, pl.ds(r, 1), :]
                        for w in range(1, 4):
                            value = value + edge_in[side, 4 + w, pl.ds(r, 1), :] * PACK[w]
                        outer.append(value.astype(jnp.int32))
                    push_masks(r, packed[r], *outer)

        @pl.when(phase == STEPS)
        def _():
            for f in range(2):
                disp_out[f] = far[f, REACH, REACH : REACH + rows].reshape(rows, segments * LANES)
                half_out[f] = half[STEPS - 1, f].reshape(rows, segments * LANES)

        @pl.when(phase > 0)
        def _():
            for c in mid_copies(phase):
                c.wait_recv()

            for r in range(rows):
                place_next(
                    r, lambda plane: half[phase - 1, plane, r],
                    lambda side, plane: edges_next[phase - 1, side, plane, r : r + 1, :],
                )

        inner_forces()

        @pl.when(phase == 0)
        def _():
            for c in rest_copies(None):
                c.wait_recv()

            for along in (0, 1):
                for k in range(REACH):
                    place_first(
                        along * (rows + REACH) - REACH + k, lambda plane: rows_in[along, plane, k],
                        lambda side, plane: corner_in[
                            along, side, plane * REACH + k : plane * REACH + k + 1, :
                        ],
                    )

            for r in range(-REACH, 0):
                word = jnp.zeros((segments, LANES), jnp.float32)
                outer = [jnp.zeros((1, LANES), jnp.float32) for side in (0, 1)]
                for a in range(-r, REACH + 1):
                    slot = row_bond_slots[(a, r)]
                    at = corner_state + slot
                    word = word + row_bonds_in[slot] * PACK[a]
                    for side in (0, 1):
                        outer[side] += corner_in[0, side, at : at + 1, :] * PACK[a]
                push_masks(r, word.astype(jnp.int32), *[x.astype(jnp.int32) for x in outer])

        @pl.when(phase > 0)
        def _():
            for c in rest_copies(phase):
                c.wait_recv()

            for along in (0, 1):
                for k in range(REACH):
                    place_next(
                        along * (rows + REACH) - REACH + k,
                        lambda plane: rows_next[phase - 1, along, plane, k],
                        lambda side, plane: corners_next[
                            phase - 1, along, side, plane * REACH + k : plane * REACH + k + 1, :
                        ],
                    )

        outer_forces(phase)

        @pl.when(phase < STEPS)
        def _():
            for c in mid_copies(phase + 1) + [row_copy(phase + 1, side) for side in (0, 1)]:
                c.start()
            for along in (0, 1):
                for across in (0, 1):
                    for f in range(2):
                        r = along * (rows - REACH)
                        corners_out[phase, along, across, f * REACH : (f + 1) * REACH, :] = (
                            edges_out[phase, across, f, r : r + REACH, :]
                        )
                    corner_copy(phase + 1, along, across).start()

    for f in range(2):
        accel_out[f] = total[f].reshape(rows, segments * LANES)
    for phase in [None, *range(1, STEPS + 1)]:
        for c in mid_copies(phase) + rest_copies(phase):
            c.wait_send()


def per_device(disp, vel, bonds):
    rows, columns = disp.shape[1:]
    segments = columns // LANES
    padded = rows + 2 * REACH
    vmem = lambda *shape: pltpu.VMEM(shape, jnp.float32)
    bond_slots = REACH * (REACH + 1) // 2
    spec = pl.BlockSpec(memory_space=pltpu.VMEM)
    earlier, half, accel = pl.pallas_call(
        kernel,
        out_shape=(jax.ShapeDtypeStruct(disp.shape, disp.dtype),) * 3,
        in_specs=[pl.BlockSpec(memory_space=pltpu.HBM)] * 3,
        out_specs=(spec,) * 3,
        scratch_shapes=[
            vmem(4, rows, columns),
            pltpu.VMEM((4, rows, columns), jnp.int32),
            vmem(4, rows, segments, LANES),
            vmem(4, len(SHIFTS), padded, segments, LANES),
            vmem(STEPS + 1, 2, rows, segments, LANES),
            pltpu.VMEM((rows, segments, LANES), jnp.int32),
            vmem(len(SHIFTS) ** 2, padded, segments, LANES),
            vmem(2, rows, segments, LANES),
            vmem(bond_slots, segments, LANES),
            vmem(2, 8, rows, LANES),
            vmem(STEPS + 1, 2, 2, rows, LANES),
            vmem(2, 2, 24, LANES),
            vmem(STEPS, 2, 2, 8, LANES),
            vmem(2, 4, REACH, segments, LANES),
            vmem(bond_slots, segments, LANES),
            vmem(2, 8, rows, LANES),
            vmem(2, 2, 24, LANES),
            vmem(STEPS, 2, 2, REACH, segments, LANES),
            vmem(STEPS, 2, 2, rows, LANES),
            vmem(STEPS, 2, 2, 8, LANES),
            pltpu.SemaphoreType.DMA((3,)),
            pltpu.SemaphoreType.DMA((STEPS + 1, 9)),
            pltpu.SemaphoreType.DMA((STEPS + 1, 9)),
        ],
        compiler_params=pltpu.CompilerParams(
            collective_id=0, has_side_effects=True, vmem_limit_bytes=55040 * 1024
        ),
    )(disp, vel, bonds)
    return earlier + TIME_STEP * half, half + 0.5 * TIME_STEP * accel


def solution(mesh):
    spec = P(None, "gx", "gy")
    return jax.shard_map(
        per_device, mesh=mesh, in_specs=(spec,) * 3, out_specs=(spec,) * 2, check_vma=False
    )
```

```python
import functools
import math

import jax
import jax.numpy as jnp
from jax import lax
from jax.experimental import pallas as pl
from jax.experimental.pallas import tpu as pltpu
from jax.sharding import PartitionSpec as P

STEPS = 2
STIFFNESS = 40.0
DAMPING = 1.0
TIME_STEP = 0.05
SOFTENING = 0.0625
REACH = 3
LANES = 128
GROUP = 2
PACK = (1, 8, 1024, 131072)
PACK_SHIFT = (0, 3, 10, 17)
MESH = pl.DeviceIdType.MESH
SHIFTS = tuple(range(-REACH, REACH + 1))


def bond_bit(a, b):
    return b - 1 if a == 0 else PACK_SHIFT[a] + b + REACH


OFFSETS = [(a, b) for a in SHIFTS for b in SHIFTS if (a, b) != (0, 0)]


def in_table(a, b):
    return a > 0 or (a == 0 and b > 0)


def spread(x, low, high, segment, lane):
    segments = x.shape[0]
    after = jnp.where(segment == segments - 1, high, pltpu.roll(x, segments - 1, 0))
    before = jnp.where(segment == 0, low, pltpu.roll(x, 1, 0))
    out = {0: x}
    for b in range(1, REACH + 1):
        out[b] = pltpu.roll(jnp.where(lane < b, after, x), LANES - b, 1)
        out[-b] = pltpu.roll(jnp.where(lane >= LANES - b, before, x), b, 1)
    return out


def kernel(
    disp_ref, vel_ref, bonds_ref, disp_out, half_out, accel_out,
    given, given_bonds, state, far, half, packed, masks, total, bond_rows, edge_out, edges_out,
    corner_out, corners_out, rows_in, row_bonds_in, edge_in, corner_in, rows_next, edges_next,
    corners_next, load, send, recv,
):
    rows = disp_ref.shape[1]
    segments = disp_ref.shape[2] // LANES
    groups = rows // GROUP
    assert rows % GROUP == 0 and groups >= 4
    corner_rows = corner_out.shape[2]
    corner_state = 16
    loads = [
        pltpu.make_async_copy(disp_ref, given.at[0:2], load.at[0]),
        pltpu.make_async_copy(vel_ref, given.at[2:4], load.at[1]),
        pltpu.make_async_copy(bonds_ref, given_bonds, load.at[2]),
    ]
    for c in loads:
        c.start()

    gx, gy = lax.axis_index("gx"), lax.axis_index("gy")
    nx, ny = lax.axis_size("gx"), lax.axis_size("gy")
    gx_at = {-1: lax.rem(gx + nx - 1, nx), 0: gx, 1: lax.rem(gx + 1, nx)}
    gy_at = {-1: lax.rem(gy + ny - 1, ny), 0: gy, 1: lax.rem(gy + 1, ny)}
    around = [(x, y) for x in (-1, 0, 1) for y in (-1, 0, 1) if (x, y) != (0, 0)]

    barrier = pltpu.get_barrier_semaphore()
    for x, y in around:
        pl.semaphore_signal(
            barrier, inc=1, device_id=(gx_at[x], gy_at[y]), device_id_type=MESH
        )

    def remote(phase, index, src, dst, x, y):
        return pltpu.make_async_remote_copy(
            src_ref=src, dst_ref=dst, send_sem=send.at[phase, index],
            recv_sem=recv.at[phase, index], device_id=(x, y), device_id_type=MESH,
        )

    def row_copy(phase, side):
        start = pl.ds(side * (rows - REACH), REACH)
        x = lax.rem(gx + nx - 1 + 2 * side, nx)
        if phase is None:
            return remote(0, side, state.at[:, start], rows_in.at[1 - side], x, gy)
        return remote(
            phase, side, half.at[phase - 1, :, start], rows_next.at[phase - 1, 1 - side], x, gy
        )

    def bond_copy():
        return remote(0, 2, bond_rows, row_bonds_in, gx_at[1], gy)

    def edge_copy(phase, side):
        y = gy_at[2 * side - 1]
        if phase is None:
            return remote(0, 3 + side, edge_out.at[side], edge_in.at[1 - side], gx, y)
        return remote(
            phase, 3 + side, edges_out.at[phase - 1, side], edges_next.at[phase - 1, 1 - side], gx, y
        )

    def corner_copy(phase, along, across, first_rows=0):
        x = lax.rem(gx + nx - 1 + 2 * along, nx)
        y = gy_at[2 * across - 1]
        index = 5 + 2 * along + across
        if phase is None:
            part = pl.ds(0, first_rows)
            return remote(
                0, index, corner_out.at[along, across, part],
                corner_in.at[1 - along, 1 - across, part], x, y,
            )
        return remote(
            phase, index, corners_out.at[phase - 1, along, across],
            corners_next.at[phase - 1, 1 - along, 1 - across], x, y,
        )

    def mid_copies(phase):
        return [edge_copy(phase, side) for side in (0, 1)]

    def rest_copies(phase):
        out = [row_copy(phase, side) for side in (0, 1)]
        if phase is None:
            out.append(bond_copy())
        return out + [
            corner_copy(phase, along, across, (corner_state, corner_rows)[along])
            for along in (0, 1) for across in (0, 1)
        ]

    def by_segments(block):
        return block.reshape(rows, segments, LANES)

    last = (segments - 1) * LANES
    loads[0].wait()
    loads[1].wait()
    for plane in range(4):
        block = given[plane]
        state[plane] = by_segments(block)
        edge_out[0, plane] = block[:, 0:LANES]
        edge_out[1, plane] = block[:, last : last + LANES]
        for along in (0, 1):
            top = along * (rows - REACH)
            at = slice(plane * REACH, (plane + 1) * REACH)
            corner_out[along, 0, at] = block[top : top + REACH, 0:LANES]
            corner_out[along, 1, at] = block[top : top + REACH, last : last + LANES]
    loads[2].wait()
    words = []
    for w in range(4):
        word = given_bonds[w].astype(jnp.float32)
        edge_out[0, 4 + w] = word[:, 0:LANES]
        edge_out[1, 4 + w] = word[:, last : last + LANES]
        words.append(by_segments(word))
    slot = 0
    row_bond_slots = {}
    for a in range(1, REACH + 1):
        for r in range(rows - a, rows):
            bond_rows[slot] = words[a][r]
            for across in (0, 1):
                at = corner_state + slot
                corner_out[1, across, at : at + 1] = edge_out[across, 4 + a, r : r + 1]
            row_bond_slots[(a, r - rows)] = slot
            slot += 1
    pl.semaphore_wait(barrier, len(around))
    for c in mid_copies(None) + rest_copies(None):
        c.start()
    own_packed = words[0] * PACK[0] + words[1] * PACK[1] + words[2] * PACK[2] + words[3] * PACK[3]
    packed[...] = own_packed.astype(jnp.int32)

    segment = lax.broadcasted_iota(jnp.int32, (segments, LANES), 0)
    lane = lax.broadcasted_iota(jnp.int32, (segments, LANES), 1)

    def mask_index(a, b):
        return (a + REACH) * len(SHIFTS) + b + REACH

    def mask(word, bit, a, b):
        return jnp.where(jnp.bitwise_and(word, 1 << bit) != 0, 1.0 / (a * a + b * b), 0.0)

    def push_masks(r, word, low, high):
        for b, value in spread(word, low, high, segment, lane).items():
            for a in range(REACH + 1):
                if in_table(a, -b):
                    masks[mask_index(-a, b), r + REACH + a] = mask(value, bond_bit(a, -b), a, b)

    def place_first(r, rows_of, outer):
        for plane in range(4):
            low, high = outer(0, plane), outer(1, plane)
            for b, value in spread(rows_of(plane), low, high, segment, lane).items():
                far[plane, b + REACH, r + REACH] = value + float(b) if plane == 1 and b else value

    def place_next(r, rows_of, outer):
        for plane in range(2):
            low, high = outer(0, plane), outer(1, plane)
            for b, value in spread(rows_of(plane), low, high, segment, lane).items():
                far[2 + plane, b + REACH, r + REACH] = value
                far[plane, b + REACH, r + REACH] += TIME_STEP * value

    @pl.loop(0, rows)
    def _(r):
        word = packed[r]
        for a, b in OFFSETS:
            if in_table(a, b):
                masks[mask_index(a, b), r + REACH] = mask(word, bond_bit(a, b), a, b)

    def evaluate(near, top, signed, sums):
        force_x, force_y = sums
        for a, size in signed:
            near_x = near[0] - float(a)
            at = pl.ds(top + REACH + a, GROUP)
            for b in SHIFTS:
                if size == 0 and b == 0:
                    continue
                rest = STIFFNESS * math.sqrt(size * size + b * b + SOFTENING)
                along_x = far[0, b + REACH, at] - near_x
                along_y = far[1, b + REACH, at] - near[1]
                speed_x = far[2, b + REACH, at] - near[2]
                speed_y = far[3, b + REACH, at] - near[3]
                inverse = lax.rsqrt(along_x * along_x + (along_y * along_y + SOFTENING))
                closing = (along_x * speed_x + along_y * speed_y) * inverse
                if DAMPING != 1.0:
                    closing = closing * DAMPING
                tension = masks[mask_index(a, b), pl.ds(top + REACH, GROUP)] * (
                    STIFFNESS - inverse * (rest - closing)
                )
                force_x += tension * along_x
                force_y += tension * along_y
        return force_x, force_y

    def near_of(top):
        return [far[f, REACH, pl.ds(top + REACH, GROUP)] for f in range(4)]

    zero = jnp.zeros((GROUP, segments, LANES), jnp.float32)

    def inner_forces():
        for side in (0, 1):
            sign = 1 - 2 * side
            for depth, sizes in ((0, range(0, REACH + 1)), (1, range(-2, REACH + 1))):
                top = depth * GROUP + side * (rows - (2 * depth + 1) * GROUP)
                signed = [(sign * a, abs(a)) for a in sizes]
                sums = evaluate(near_of(top), top, signed, (zero, zero))
                for f in range(2):
                    total[f, pl.ds(top, GROUP)] = sums[f]

        if groups > 4:
            @pl.loop(2, groups - 2)
            def _(group):
                top = group * GROUP
                sums = evaluate(near_of(top), top, [(a, abs(a)) for a in SHIFTS], (zero, zero))
                for f in range(2):
                    total[f, pl.ds(top, GROUP)] = sums[f]

    def kicked(phase, top, near, sums):
        again = jnp.where(jnp.logical_and(phase > 0, phase < STEPS), 1.0, 0.0)
        for f in range(2):
            kick = (0.5 * TIME_STEP) * sums[f]
            value = (near[2 + f] + kick) + kick * again
            half[phase, f, pl.ds(top, GROUP)] = value
            total[f, pl.ds(top, GROUP)] = sums[f]
            for k in range(GROUP):
                edges_out[phase, 0, f, pl.ds(top + k, 1), :] = value[k, 0:1]
                edges_out[phase, 1, f, pl.ds(top + k, 1), :] = value[k, segments - 1 : segments]

    def arrive(phase, side):
        first = side * (rows + REACH) - REACH

        @pl.when(phase == 0)
        def _():
            row_copy(None, 1 - side).wait_recv()
            for across in (0, 1):
                corner_copy(
                    None, 1 - side, across, (corner_state, corner_rows)[1 - side]
                ).wait_recv()
            for k in range(REACH):
                place_first(
                    first + k, lambda plane: rows_in[side, plane, k],
                    lambda across, plane: corner_in[
                        side, across, plane * REACH + k : plane * REACH + k + 1, :
                    ],
                )
            if side == 0:
                bond_copy().wait_recv()
                for r in range(-REACH, 0):
                    word = jnp.zeros((segments, LANES), jnp.float32)
                    outer = [jnp.zeros((1, LANES), jnp.float32) for across in (0, 1)]
                    for a in range(-r, REACH + 1):
                        slot = row_bond_slots[(a, r)]
                        at = corner_state + slot
                        word = word + row_bonds_in[slot] * PACK[a]
                        for across in (0, 1):
                            outer[across] += corner_in[0, across, at : at + 1, :] * PACK[a]
                    push_masks(r, word.astype(jnp.int32), *[x.astype(jnp.int32) for x in outer])

        @pl.when(phase > 0)
        def _():
            row_copy(phase, 1 - side).wait_recv()
            for across in (0, 1):
                corner_copy(phase, 1 - side, across).wait_recv()
            for k in range(REACH):
                place_next(
                    first + k, lambda plane: rows_next[phase - 1, side, plane, k],
                    lambda across, plane: corners_next[
                        phase - 1, side, across, plane * REACH + k : plane * REACH + k + 1, :
                    ],
                )

    def outer_forces(phase):
        if groups > 4:
            @pl.loop(2, groups - 2)
            def _(group):
                top = group * GROUP
                kicked(phase, top, near_of(top), [total[f, pl.ds(top, GROUP)] for f in range(2)])

        for side in (0, 1):
            arrive(phase, side)
            sign = 1 - 2 * side
            for depth, sizes in ((0, (-1, -2, -3)), (1, (-3,))):
                top = depth * GROUP + side * (rows - (2 * depth + 1) * GROUP)
                near = near_of(top)
                sums = [total[f, pl.ds(top, GROUP)] for f in range(2)]
                signed = [(sign * a, abs(a)) for a in sizes]
                kicked(phase, top, near, evaluate(near, top, signed, sums))
            if side == 0:
                @pl.when(phase < STEPS)
                def _():
                    row_copy(phase + 1, 0).start()

    @pl.loop(0, STEPS + 1)
    def _(phase):
        @pl.when(phase == 0)
        def _():
            for c in mid_copies(None):
                c.wait_recv()

            @pl.loop(0, groups // 2)
            def _(group):
                for k in range(2 * GROUP):
                    r = group * (2 * GROUP) + k
                    place_first(
                        r, lambda plane: state[plane, r],
                        lambda side, plane: edge_in[side, plane, pl.ds(r, 1), :],
                    )
                    outer = []
                    for side in (0, 1):
                        value = edge_in[side, 4, pl.ds(r, 1), :]
                        for w in range(1, 4):
                            value = value + edge_in[side, 4 + w, pl.ds(r, 1), :] * PACK[w]
                        outer.append(value.astype(jnp.int32))
                    push_masks(r, packed[r], *outer)

        @pl.when(phase == STEPS)
        def _():
            for f in range(2):
                disp_out[f] = far[f, REACH, REACH : REACH + rows].reshape(rows, segments * LANES)
                half_out[f] = half[STEPS - 1, f].reshape(rows, segments * LANES)

        @pl.when(phase > 0)
        def _():
            for c in mid_copies(phase):
                c.wait_recv()

            for r in range(rows):
                place_next(
                    r, lambda plane: half[phase - 1, plane, r],
                    lambda side, plane: edges_next[phase - 1, side, plane, r : r + 1, :],
                )

        inner_forces()

        outer_forces(phase)

        @pl.when(phase < STEPS)
        def _():
            for c in mid_copies(phase + 1) + [row_copy(phase + 1, 1)]:
                c.start()
            for along in (0, 1):
                for across in (0, 1):
                    for f in range(2):
                        r = along * (rows - REACH)
                        corners_out[phase, along, across, f * REACH : (f + 1) * REACH, :] = (
                            edges_out[phase, across, f, r : r + REACH, :]
                        )
                    corner_copy(phase + 1, along, across).start()

    for f in range(2):
        accel_out[f] = total[f].reshape(rows, segments * LANES)
    for phase in [None, *range(1, STEPS + 1)]:
        for c in mid_copies(phase) + rest_copies(phase):
            c.wait_send()


def per_device(disp, vel, bonds):
    rows, columns = disp.shape[1:]
    segments = columns // LANES
    padded = rows + 2 * REACH
    vmem = lambda *shape: pltpu.VMEM(shape, jnp.float32)
    bond_slots = REACH * (REACH + 1) // 2
    spec = pl.BlockSpec(memory_space=pltpu.VMEM)
    earlier, half, accel = pl.pallas_call(
        kernel,
        out_shape=(jax.ShapeDtypeStruct(disp.shape, disp.dtype),) * 3,
        in_specs=[pl.BlockSpec(memory_space=pltpu.HBM)] * 3,
        out_specs=(spec,) * 3,
        scratch_shapes=[
            vmem(4, rows, columns),
            pltpu.VMEM((4, rows, columns), jnp.int32),
            vmem(4, rows, segments, LANES),
            vmem(4, len(SHIFTS), padded, segments, LANES),
            vmem(STEPS + 1, 2, rows, segments, LANES),
            pltpu.VMEM((rows, segments, LANES), jnp.int32),
            vmem(len(SHIFTS) ** 2, padded, segments, LANES),
            vmem(2, rows, segments, LANES),
            vmem(bond_slots, segments, LANES),
            vmem(2, 8, rows, LANES),
            vmem(STEPS + 1, 2, 2, rows, LANES),
            vmem(2, 2, 24, LANES),
            vmem(STEPS, 2, 2, 8, LANES),
            vmem(2, 4, REACH, segments, LANES),
            vmem(bond_slots, segments, LANES),
            vmem(2, 8, rows, LANES),
            vmem(2, 2, 24, LANES),
            vmem(STEPS, 2, 2, REACH, segments, LANES),
            vmem(STEPS, 2, 2, rows, LANES),
            vmem(STEPS, 2, 2, 8, LANES),
            pltpu.SemaphoreType.DMA((3,)),
            pltpu.SemaphoreType.DMA((STEPS + 1, 9)),
            pltpu.SemaphoreType.DMA((STEPS + 1, 9)),
        ],
        compiler_params=pltpu.CompilerParams(
            collective_id=0, has_side_effects=True, vmem_limit_bytes=55040 * 1024
        ),
    )(disp, vel, bonds)
    return earlier + TIME_STEP * half, half + 0.5 * TIME_STEP * accel


def solution(mesh):
    spec = P(None, "gx", "gy")
    return jax.shard_map(
        per_device, mesh=mesh, in_specs=(spec,) * 3, out_specs=(spec,) * 2, check_vma=False
    )
```

```python
import functools
import math

import jax
import jax.numpy as jnp
from jax import lax
from jax.experimental import pallas as pl
from jax.experimental.pallas import tpu as pltpu
from jax.sharding import PartitionSpec as P

STEPS = 2
STIFFNESS = 40.0
DAMPING = 1.0
TIME_STEP = 0.05
SOFTENING = 0.0625
REACH = 3
LANES = 128
GROUP = 2
PACK = (1, 8, 1024, 131072)
PACK_SHIFT = (0, 3, 10, 17)
MESH = pl.DeviceIdType.MESH
SHIFTS = tuple(range(-REACH, REACH + 1))


def bond_bit(a, b):
    return b - 1 if a == 0 else PACK_SHIFT[a] + b + REACH


OFFSETS = [(a, b) for a in SHIFTS for b in SHIFTS if (a, b) != (0, 0)]


def in_table(a, b):
    return a > 0 or (a == 0 and b > 0)


def spread(x, low, high, segment, lane):
    segments = x.shape[0]
    after = jnp.where(segment == segments - 1, high, pltpu.roll(x, segments - 1, 0))
    before = jnp.where(segment == 0, low, pltpu.roll(x, 1, 0))
    out = {0: x}
    for b in range(1, REACH + 1):
        out[b] = pltpu.roll(jnp.where(lane < b, after, x), LANES - b, 1)
        out[-b] = pltpu.roll(jnp.where(lane >= LANES - b, before, x), b, 1)
    return out


def kernel(
    disp_ref, vel_ref, bonds_ref, disp_out, half_out, accel_out,
    given, given_bonds, state, far, half, packed, masks, total, bond_rows, edge_out, edges_out,
    corner_out, corners_out, rows_in, row_bonds_in, edge_in, corner_in, rows_next, edges_next,
    corners_next, load, send, recv,
):
    rows = disp_ref.shape[1]
    segments = disp_ref.shape[2] // LANES
    groups = rows // GROUP
    assert rows % GROUP == 0 and groups >= 4
    corner_rows = corner_out.shape[2]
    corner_state = 16
    loads = [
        pltpu.make_async_copy(disp_ref, given.at[0:2], load.at[0]),
        pltpu.make_async_copy(vel_ref, given.at[2:4], load.at[1]),
        pltpu.make_async_copy(bonds_ref, given_bonds, load.at[2]),
    ]
    for c in loads:
        c.start()

    gx, gy = lax.axis_index("gx"), lax.axis_index("gy")
    nx, ny = lax.axis_size("gx"), lax.axis_size("gy")
    gx_at = {-1: lax.rem(gx + nx - 1, nx), 0: gx, 1: lax.rem(gx + 1, nx)}
    gy_at = {-1: lax.rem(gy + ny - 1, ny), 0: gy, 1: lax.rem(gy + 1, ny)}
    around = [(x, y) for x in (-1, 0, 1) for y in (-1, 0, 1) if (x, y) != (0, 0)]

    barrier = pltpu.get_barrier_semaphore()
    for x, y in around:
        pl.semaphore_signal(
            barrier, inc=1, device_id=(gx_at[x], gy_at[y]), device_id_type=MESH
        )

    def remote(phase, index, src, dst, x, y):
        return pltpu.make_async_remote_copy(
            src_ref=src, dst_ref=dst, send_sem=send.at[phase, index],
            recv_sem=recv.at[phase, index], device_id=(x, y), device_id_type=MESH,
        )

    def row_copy(phase, side):
        start = pl.ds(side * (rows - REACH), REACH)
        x = lax.rem(gx + nx - 1 + 2 * side, nx)
        if phase is None:
            return remote(0, side, state.at[:, start], rows_in.at[1 - side], x, gy)
        return remote(
            phase, side, half.at[phase - 1, :, start], rows_next.at[phase - 1, 1 - side], x, gy
        )

    def bond_copy():
        return remote(0, 2, bond_rows, row_bonds_in, gx_at[1], gy)

    def edge_copy(phase, side):
        y = gy_at[2 * side - 1]
        if phase is None:
            return remote(0, 3 + side, edge_out.at[side], edge_in.at[1 - side], gx, y)
        return remote(
            phase, 3 + side, edges_out.at[phase - 1, side], edges_next.at[phase - 1, 1 - side], gx, y
        )

    def corner_copy(phase, along, across, first_rows=0):
        x = lax.rem(gx + nx - 1 + 2 * along, nx)
        y = gy_at[2 * across - 1]
        index = 5 + 2 * along + across
        if phase is None:
            part = pl.ds(0, first_rows)
            return remote(
                0, index, corner_out.at[along, across, part],
                corner_in.at[1 - along, 1 - across, part], x, y,
            )
        return remote(
            phase, index, corners_out.at[phase - 1, along, across],
            corners_next.at[phase - 1, 1 - along, 1 - across], x, y,
        )

    def mid_copies(phase):
        return [edge_copy(phase, side) for side in (0, 1)]

    def rest_copies(phase):
        out = [row_copy(phase, side) for side in (0, 1)]
        if phase is None:
            out.append(bond_copy())
        return out + [
            corner_copy(phase, along, across, (corner_state, corner_rows)[along])
            for along in (0, 1) for across in (0, 1)
        ]

    def by_segments(block):
        return block.reshape(rows, segments, LANES)

    last = (segments - 1) * LANES
    loads[0].wait()
    loads[1].wait()
    for plane in range(4):
        block = given[plane]
        state[plane] = by_segments(block)
        edge_out[0, plane] = block[:, 0:LANES]
        edge_out[1, plane] = block[:, last : last + LANES]
        for along in (0, 1):
            top = along * (rows - REACH)
            at = slice(plane * REACH, (plane + 1) * REACH)
            corner_out[along, 0, at] = block[top : top + REACH, 0:LANES]
            corner_out[along, 1, at] = block[top : top + REACH, last : last + LANES]
    pl.semaphore_wait(barrier, len(around))
    for side in (0, 1):
        row_copy(None, side).start()
    loads[2].wait()
    words = []
    for w in range(4):
        word = given_bonds[w].astype(jnp.float32)
        edge_out[0, 4 + w] = word[:, 0:LANES]
        edge_out[1, 4 + w] = word[:, last : last + LANES]
        words.append(by_segments(word))
    slot = 0
    row_bond_slots = {}
    for a in range(1, REACH + 1):
        for r in range(rows - a, rows):
            bond_rows[slot] = words[a][r]
            for across in (0, 1):
                at = corner_state + slot
                corner_out[1, across, at : at + 1] = edge_out[across, 4 + a, r : r + 1]
            row_bond_slots[(a, r - rows)] = slot
            slot += 1
    for c in mid_copies(None) + rest_copies(None)[2:]:
        c.start()
    own_packed = words[0] * PACK[0] + words[1] * PACK[1] + words[2] * PACK[2] + words[3] * PACK[3]
    packed[...] = own_packed.astype(jnp.int32)

    segment = lax.broadcasted_iota(jnp.int32, (segments, LANES), 0)
    lane = lax.broadcasted_iota(jnp.int32, (segments, LANES), 1)

    def mask_index(a, b):
        return (a + REACH) * len(SHIFTS) + b + REACH

    def mask(word, bit, a, b):
        return jnp.where(jnp.bitwise_and(word, 1 << bit) != 0, 1.0 / (a * a + b * b), 0.0)

    def push_masks(r, word, low, high):
        for b, value in spread(word, low, high, segment, lane).items():
            for a in range(REACH + 1):
                if in_table(a, -b):
                    masks[mask_index(-a, b), r + REACH + a] = mask(value, bond_bit(a, -b), a, b)

    def place_first(r, rows_of, outer):
        for plane in range(4):
            low, high = outer(0, plane), outer(1, plane)
            for b, value in spread(rows_of(plane), low, high, segment, lane).items():
                far[plane, b + REACH, r + REACH] = value + float(b) if plane == 1 and b else value

    def place_next(r, rows_of, outer):
        for plane in range(2):
            low, high = outer(0, plane), outer(1, plane)
            for b, value in spread(rows_of(plane), low, high, segment, lane).items():
                far[2 + plane, b + REACH, r + REACH] = value
                far[plane, b + REACH, r + REACH] += TIME_STEP * value

    @pl.loop(0, rows)
    def _(r):
        word = packed[r]
        for a, b in OFFSETS:
            if in_table(a, b):
                masks[mask_index(a, b), r + REACH] = mask(word, bond_bit(a, b), a, b)

    def evaluate(near, top, signed, sums):
        force_x, force_y = sums
        for a, size in signed:
            near_x = near[0] - float(a)
            at = pl.ds(top + REACH + a, GROUP)
            for b in SHIFTS:
                if size == 0 and b == 0:
                    continue
                rest = STIFFNESS * math.sqrt(size * size + b * b + SOFTENING)
                along_x = far[0, b + REACH, at] - near_x
                along_y = far[1, b + REACH, at] - near[1]
                speed_x = far[2, b + REACH, at] - near[2]
                speed_y = far[3, b + REACH, at] - near[3]
                inverse = lax.rsqrt(along_x * along_x + (along_y * along_y + SOFTENING))
                closing = (along_x * speed_x + along_y * speed_y) * inverse
                if DAMPING != 1.0:
                    closing = closing * DAMPING
                tension = masks[mask_index(a, b), pl.ds(top + REACH, GROUP)] * (
                    STIFFNESS - inverse * (rest - closing)
                )
                force_x += tension * along_x
                force_y += tension * along_y
        return force_x, force_y

    def near_of(top):
        return [far[f, REACH, pl.ds(top + REACH, GROUP)] for f in range(4)]

    zero = jnp.zeros((GROUP, segments, LANES), jnp.float32)

    def inner_forces():
        for side in (0, 1):
            sign = 1 - 2 * side
            for depth, sizes in ((0, range(0, REACH + 1)), (1, range(-2, REACH + 1))):
                top = depth * GROUP + side * (rows - (2 * depth + 1) * GROUP)
                signed = [(sign * a, abs(a)) for a in sizes]
                sums = evaluate(near_of(top), top, signed, (zero, zero))
                for f in range(2):
                    total[f, pl.ds(top, GROUP)] = sums[f]

        if groups > 4:
            @pl.loop(2, groups - 2)
            def _(group):
                top = group * GROUP
                sums = evaluate(near_of(top), top, [(a, abs(a)) for a in SHIFTS], (zero, zero))
                for f in range(2):
                    total[f, pl.ds(top, GROUP)] = sums[f]

    def kicked(phase, top, near, sums):
        again = jnp.where(jnp.logical_and(phase > 0, phase < STEPS), 1.0, 0.0)
        for f in range(2):
            kick = (0.5 * TIME_STEP) * sums[f]
            value = (near[2 + f] + kick) + kick * again
            half[phase, f, pl.ds(top, GROUP)] = value
            total[f, pl.ds(top, GROUP)] = sums[f]
            for k in range(GROUP):
                edges_out[phase, 0, f, pl.ds(top + k, 1), :] = value[k, 0:1]
                edges_out[phase, 1, f, pl.ds(top + k, 1), :] = value[k, segments - 1 : segments]

    def arrive(phase, side):
        first = side * (rows + REACH) - REACH

        @pl.when(phase == 0)
        def _():
            row_copy(None, 1 - side).wait_recv()
            for across in (0, 1):
                corner_copy(
                    None, 1 - side, across, (corner_state, corner_rows)[1 - side]
                ).wait_recv()
            for k in range(REACH):
                place_first(
                    first + k, lambda plane: rows_in[side, plane, k],
                    lambda across, plane: corner_in[
                        side, across, plane * REACH + k : plane * REACH + k + 1, :
                    ],
                )
            if side == 0:
                bond_copy().wait_recv()
                for r in range(-REACH, 0):
                    word = jnp.zeros((segments, LANES), jnp.float32)
                    outer = [jnp.zeros((1, LANES), jnp.float32) for across in (0, 1)]
                    for a in range(-r, REACH + 1):
                        slot = row_bond_slots[(a, r)]
                        at = corner_state + slot
                        word = word + row_bonds_in[slot] * PACK[a]
                        for across in (0, 1):
                            outer[across] += corner_in[0, across, at : at + 1, :] * PACK[a]
                    push_masks(r, word.astype(jnp.int32), *[x.astype(jnp.int32) for x in outer])

        @pl.when(phase > 0)
        def _():
            row_copy(phase, 1 - side).wait_recv()
            for across in (0, 1):
                corner_copy(phase, 1 - side, across).wait_recv()
            for k in range(REACH):
                place_next(
                    first + k, lambda plane: rows_next[phase - 1, side, plane, k],
                    lambda across, plane: corners_next[
                        phase - 1, side, across, plane * REACH + k : plane * REACH + k + 1, :
                    ],
                )

    def outer_forces(phase):
        if groups > 4:
            @pl.loop(2, groups - 2)
            def _(group):
                top = group * GROUP
                kicked(phase, top, near_of(top), [total[f, pl.ds(top, GROUP)] for f in range(2)])

        for side in (0, 1):
            arrive(phase, side)
            sign = 1 - 2 * side
            for depth, sizes in ((0, (-1, -2, -3)), (1, (-3,))):
                top = depth * GROUP + side * (rows - (2 * depth + 1) * GROUP)
                near = near_of(top)
                sums = [total[f, pl.ds(top, GROUP)] for f in range(2)]
                signed = [(sign * a, abs(a)) for a in sizes]
                kicked(phase, top, near, evaluate(near, top, signed, sums))
            if side == 0:
                @pl.when(phase < STEPS)
                def _():
                    row_copy(phase + 1, 0).start()

    @pl.loop(0, STEPS + 1)
    def _(phase):
        @pl.when(phase == 0)
        def _():
            for c in mid_copies(None):
                c.wait_recv()

            @pl.loop(0, groups // 2)
            def _(group):
                for k in range(2 * GROUP):
                    r = group * (2 * GROUP) + k
                    place_first(
                        r, lambda plane: state[plane, r],
                        lambda side, plane: edge_in[side, plane, pl.ds(r, 1), :],
                    )
                    outer = []
                    for side in (0, 1):
                        value = edge_in[side, 4, pl.ds(r, 1), :]
                        for w in range(1, 4):
                            value = value + edge_in[side, 4 + w, pl.ds(r, 1), :] * PACK[w]
                        outer.append(value.astype(jnp.int32))
                    push_masks(r, packed[r], *outer)

        @pl.when(phase == STEPS)
        def _():
            for f in range(2):
                disp_out[f] = far[f, REACH, REACH : REACH + rows].reshape(rows, segments * LANES)
                half_out[f] = half[STEPS - 1, f].reshape(rows, segments * LANES)

        @pl.when(phase > 0)
        def _():
            for c in mid_copies(phase):
                c.wait_recv()

            for r in range(rows):
                place_next(
                    r, lambda plane: half[phase - 1, plane, r],
                    lambda side, plane: edges_next[phase - 1, side, plane, r : r + 1, :],
                )

        inner_forces()

        outer_forces(phase)

        @pl.when(phase < STEPS)
        def _():
            for c in mid_copies(phase + 1) + [row_copy(phase + 1, 1)]:
                c.start()
            for along in (0, 1):
                for across in (0, 1):
                    for f in range(2):
                        r = along * (rows - REACH)
                        corners_out[phase, along, across, f * REACH : (f + 1) * REACH, :] = (
                            edges_out[phase, across, f, r : r + REACH, :]
                        )
                    corner_copy(phase + 1, along, across).start()

    for f in range(2):
        accel_out[f] = total[f].reshape(rows, segments * LANES)
    for phase in [None, *range(1, STEPS + 1)]:
        for c in mid_copies(phase) + rest_copies(phase):
            c.wait_send()


def per_device(disp, vel, bonds):
    rows, columns = disp.shape[1:]
    segments = columns // LANES
    padded = rows + 2 * REACH
    vmem = lambda *shape: pltpu.VMEM(shape, jnp.float32)
    bond_slots = REACH * (REACH + 1) // 2
    spec = pl.BlockSpec(memory_space=pltpu.VMEM)
    earlier, half, accel = pl.pallas_call(
        kernel,
        out_shape=(jax.ShapeDtypeStruct(disp.shape, disp.dtype),) * 3,
        in_specs=[pl.BlockSpec(memory_space=pltpu.HBM)] * 3,
        out_specs=(spec,) * 3,
        scratch_shapes=[
            vmem(4, rows, columns),
            pltpu.VMEM((4, rows, columns), jnp.int32),
            vmem(4, rows, segments, LANES),
            vmem(4, len(SHIFTS), padded, segments, LANES),
            vmem(STEPS + 1, 2, rows, segments, LANES),
            pltpu.VMEM((rows, segments, LANES), jnp.int32),
            vmem(len(SHIFTS) ** 2, padded, segments, LANES),
            vmem(2, rows, segments, LANES),
            vmem(bond_slots, segments, LANES),
            vmem(2, 8, rows, LANES),
            vmem(STEPS + 1, 2, 2, rows, LANES),
            vmem(2, 2, 24, LANES),
            vmem(STEPS, 2, 2, 8, LANES),
            vmem(2, 4, REACH, segments, LANES),
            vmem(bond_slots, segments, LANES),
            vmem(2, 8, rows, LANES),
            vmem(2, 2, 24, LANES),
            vmem(STEPS, 2, 2, REACH, segments, LANES),
            vmem(STEPS, 2, 2, rows, LANES),
            vmem(STEPS, 2, 2, 8, LANES),
            pltpu.SemaphoreType.DMA((3,)),
            pltpu.SemaphoreType.DMA((STEPS + 1, 9)),
            pltpu.SemaphoreType.DMA((STEPS + 1, 9)),
        ],
        compiler_params=pltpu.CompilerParams(
            collective_id=0, has_side_effects=True, vmem_limit_bytes=55040 * 1024
        ),
    )(disp, vel, bonds)
    return earlier + TIME_STEP * half, half + 0.5 * TIME_STEP * accel


def solution(mesh):
    spec = P(None, "gx", "gy")
    return jax.shard_map(
        per_device, mesh=mesh, in_specs=(spec,) * 3, out_specs=(spec,) * 2, check_vma=False
    )
```
